128 devices in a mesh: replica: 8 (over y_lo, x), fsdp: 16 (over z, y_hi, core).
Axes of the slice: x: 4, y: 4 (y_hi: 2, y_lo: 2; y = y_hi * 2 + y_lo), z: 4, core: 2. Of those that a mesh axis runs over, the one named last changes fastest.
Arguments:
- pseudo_grads: bfloat16 [8, 8192, 8192], P('replica', None, 'fsdp'), may hold values from -6 to 6
- exponents: int32 [8, 8192, 64], P('replica', None, 'fsdp'), may hold values from -6 to 1
- master: float32 [8192, 8192], P(('replica', 'fsdp')), may hold values from -6 to 6
- momentum: float32 [8192, 8192], P(('replica', 'fsdp')), may hold values from -4 to 4
- layout: int32 [8], replicated, may hold values from 0 to 7, each once
Outputs:
- new_master: float32 [8192, 8192], P(('replica', 'fsdp'))
- new_momentum: float32 [8192, 8192], P(('replica', 'fsdp'))
- island_params: bfloat16 [8192, 8192], P(None, 'fsdp')
The draws below stay inside these ranges and needn't reach their ends.
Inputs may be any that keep to these rules, and one draw needn't show every extreme that they name: `layout`: a permutation of the layers.
All inputs are finite; a program needn't handle non-finite values.
Results may differ from the reference program's by a relative error of at most 0.0095.
Values may be sent and summed in bfloat16 or wider, within the bound.
A program may use at most 192 MiB of HBM per device.

```python
import jax
import jax.numpy as jnp

COLS = 8192
LAYERS = 8
REPLICAS = 8
ROWS = 8192
LROWS = 1024


def set_ends(entries, stream_key, low, top_value):
    shape = entries.shape
    place = [jax.random.randint(jax.random.fold_in(stream_key, axis), (), 0, shape[axis]) for axis in range(len(shape))]
    entries = entries.at[tuple(place)].set(low)
    longest = shape.index(max(shape))
    place[longest] = (place[longest] + 1) % shape[longest]
    return entries.at[tuple(place)].set(top_value)


def raised(entries, rng, source, target, parts, factor):
    def block_of(axis_at):
        return (jnp.arange(entries.shape[axis_at]) // (entries.shape[axis_at] // parts)).reshape((-1,) + (1,) * (entries.ndim - 1 - axis_at))

    first = jax.random.permutation(rng, parts)[block_of(target)]
    far = (block_of(target) + parts // 2) % parts
    return jnp.where((block_of(source) == first) | (block_of(source) == far), factor * entries, entries)


def levels(stream_key, dims, pieces, least, top_value):
    def one(dim, parts):
        draws = jax.random.uniform(jax.random.fold_in(jax.random.fold_in(stream_key, 6), dim), (parts,), jnp.float32, least / len(pieces), top_value / len(pieces))
        return jnp.repeat(jnp.exp(draws), dims[dim] // parts).reshape((-1,) + (1,) * (len(dims) - dim - 1))

    loudness = one(*pieces[0])
    for cut in pieces[1:]:
        loudness = loudness * one(*cut)
    return loudness


def bell_draw(stream_key, extent, width, limit, shards=(), dtype=jnp.bfloat16):
    gain = levels(stream_key, extent, shards, -0.22, 0.18) if shards else 1.0
    values = jax.random.normal(stream_key, extent, jnp.float32) * width * gain
    return jnp.minimum(jnp.maximum(values, -limit), limit).astype(dtype)


def bell_draw_with(stream_key, dims, deviation, most, split, heavy, kind=jnp.bfloat16):
    drawn = deviation * jax.random.normal(stream_key, dims, jnp.float32)
    if split:
        drawn = drawn * levels(stream_key, dims, split, -0.22, 0.18)
    return jnp.clip(raised(drawn, jax.random.fold_in(stream_key, 3), *heavy), -most, most).astype(kind)


def setup_inputs(seed: int = 0) -> dict:
    arg_keys = jax.random.split(jax.random.key(seed), 6)
    return {
        "pseudo_grads": bell_draw_with(arg_keys[0], (REPLICAS, ROWS, COLS), 1.0, 6.0, ((0, 8), (2, 16)), (0, 1, 8, 2.0)),
        "exponents": set_ends(jax.random.randint(arg_keys[1], (REPLICAS, ROWS, COLS // 128), -6, 2), jax.random.fold_in(arg_keys[1], 1), -6, 1).astype(jnp.int32),
        "master": bell_draw(arg_keys[2], (ROWS, COLS), 1.0, 6.0, ((0, 128),), jnp.float32),
        "momentum": bell_draw(arg_keys[3], (ROWS, COLS), 0.5, 4.0, ((0, 128),), jnp.float32),
        "layout": jax.random.permutation(arg_keys[4], LAYERS).astype(jnp.int32),
    }


outer_rate = 0.7
outer_momentum = 0.9


def block_scale(exponents):
    scale = jnp.zeros(exponents.shape, jnp.float32)
    for level in range(-6, 2):
        scale = jnp.where(exponents == level, jnp.float32(2.0 ** level), scale)
    return scale


def decode(coded, exponents):
    shape = coded.shape
    blocks = coded.reshape(shape[:-1] + (shape[-1] // 128, 128)).astype(jnp.float32)
    return (blocks * block_scale(exponents)[..., None]).reshape(shape)


def reference(pseudo_grads, exponents, master, momentum, layout):
    total = jnp.zeros(master.shape, jnp.float32)
    for replica_index in range(REPLICAS):
        total = total + decode(pseudo_grads[replica_index], exponents[replica_index])
    average = total / jnp.float32(REPLICAS)
    new_momentum = outer_momentum * momentum + average
    new_master = master - outer_rate * (average + outer_momentum * new_momentum)
    rounded = new_master.astype(jnp.bfloat16)
    grouped = rounded.reshape(LAYERS, LROWS, COLS)
    island_params = jnp.take(grouped, layout, axis=0).reshape(ROWS, COLS)
    return new_master, new_momentum, island_params
```

```python
import jax
import jax.numpy as jnp
from jax import lax
from jax.experimental import pallas as pl
from jax.experimental.pallas import tpu as pltpu
from jax.sharding import PartitionSpec as P

MESH = pl.DeviceIdType.MESH
F32, BF16 = jnp.float32, jnp.bfloat16

outer_rate = 0.7
outer_momentum = 0.9

UNITS = 16
TILES = 16
XT = 9
XP = 5
YT = TILES - XT
YP = 3
YM = XT + YP


def bit(v, b):
    return (v // (1 << b)) % 2


def flip(a, b):
    return a + b - 2 * a * b


def xor16(f, t):
    return sum(flip(bit(f, b), bit(t, b)) * (1 << b) for b in range(4))


def block_scale(exponents):
    scale = jnp.zeros(exponents.shape, F32)
    for level in range(-6, 2):
        scale = jnp.where(exponents == level, F32(2.0**level), scale)
    return scale


def step_kernel(
    g, expt, master, momentum,
    isl, new_master, new_momentum,
    graw, dec, r1p, r1m, r1y, r2p, r2m, q2p, q2m, r3x, q3p, q3m, a2a, ret, mas, mom, omas, omom,
    g_sem, m_sem, o_sem, own_sem, rs_send, rs_recv, a_send, a_recv, b_send, b_recv, ag_send, ag_recv,
):
    rep, fs = lax.axis_index("replica"), lax.axis_index("fsdp")
    x, yl = rep % 4, rep // 4
    xp, xm, xo = (x + 1) % 4, (x + 3) % 4, (x + 2) % 4
    right, left, side = (yl * 4 + xp, fs), (yl * 4 + xm, fs), ((1 - yl) * 4 + x, fs)

    def own(t):
        return flip(yl, bit(t, 1))

    def partner(t):
        return (own(t) * 4 + x, xor16(fs, t))

    def columns(t):
        return pl.ds(pl.multiple_of(xor16(fs, t) * 512, 512), 512)

    def load_g(p):
        return pltpu.make_async_copy(g.at[:, xor16(fs, 2 * p) // 2], graw.at[p], g_sem.at[p])

    def load_m(t):
        return (
            pltpu.make_async_copy(master.at[:, columns(t)], mas.at[t], m_sem.at[0, t]),
            pltpu.make_async_copy(momentum.at[:, columns(t)], mom.at[t], m_sem.at[1, t]),
        )

    def store_m(t):
        return (
            pltpu.make_async_copy(omas.at[t], new_master.at[:, columns(t)], o_sem.at[0, t]),
            pltpu.make_async_copy(omom.at[t], new_momentum.at[:, columns(t)], o_sem.at[1, t]),
        )

    def remote(src, dst, send, recv, device):
        return pltpu.make_async_remote_copy(
            src_ref=src, dst_ref=dst, send_sem=send, recv_sem=recv, device_id=device, device_id_type=MESH
        )

    def rs(t, i):
        o = own(t)
        every = slice(None)
        src, dst, device = (
            (dec.at[t, every, xo, pl.ds(0, XP)], r1p, right),
            (dec.at[t, every, xo, pl.ds(XP, XT - XP)], r1m, left),
            (dec.at[t, 1 - o, every, pl.ds(XT, YT)], r1y, side),
            (dec.at[t, every, xp, pl.ds(0, XT)], r2p, right),
            (dec.at[t, every, xm, pl.ds(0, XT)], r2m, left),
            (dec.at[t, o, xo, pl.ds(XT, YP)], q2p, right),
            (dec.at[t, o, xo, pl.ds(YM, YT - YP)], q2m, left),
            (dec.at[t, 1 - o, x, pl.ds(0, XT)], r3x, side),
            (dec.at[t, o, xp, pl.ds(XT, YT)], q3p, right),
            (dec.at[t, o, xm, pl.ds(XT, YT)], q3m, left),
        )[i]
        return remote(src, dst.at[t], rs_send.at[t, i], rs_recv.at[t, i], device)

    def ag(t, i, arriving=False):
        o, j = own(t), xor16(fs, t)
        every = slice(None)
        cp, cm = (xm, xp) if arriving else (x, x)
        fp, fm = (xo, xo) if arriving else (xm, xp)
        mine = 1 - o if arriving else o
        ref, device = (
            (isl.at[j, mine, x, pl.ds(0, XT)], side),
            (isl.at[j, o, cp, pl.ds(XT, YT)], right),
            (isl.at[j, o, cm, pl.ds(XT, YT)], left),
            (isl.at[j, every, cp, pl.ds(0, XT)], right),
            (isl.at[j, every, cm, pl.ds(0, XT)], left),
            (isl.at[j, o, fp, pl.ds(XT, YP)], right),
            (isl.at[j, o, fm, pl.ds(YM, YT - YP)], left),
            (isl.at[j, every, fp, pl.ds(0, XP)], right),
            (isl.at[j, every, fm, pl.ds(XP, XT - XP)], left),
            (isl.at[j, mine, every, pl.ds(XT, YT)], side),
        )[i]
        return remote(ref, ref, ag_send.at[t, i], ag_recv.at[t, i], device)

    def go(t):
        return remote(dec.at[t, own(t), x], a2a.at[t], a_send.at[t], a_recv.at[t], partner(t))

    def back(t, arriving=False):
        place = isl.at[xor16(fs, t), own(t), x] if arriving else isl.at[fs, yl, x]
        return remote(ret.at[t], place, b_send.at[t], b_recv.at[t], partner(t))

    def back_own():
        return pltpu.make_async_copy(ret.at[0], isl.at[fs, yl, x], own_sem)

    def wide(ref, *at):
        return ref[at].astype(F32)

    lane_block = lax.broadcasted_iota(jnp.int32, (8, 512), 1) // 128
    pick = (lane_block == lax.broadcasted_iota(jnp.int32, (8, 512), 0)).astype(F32)

    def decode(p):
        load_g(p).wait()
        base = xor16(fs, 2 * p) // 2 * 128
        odd = fs % 2

        def one(l, _):
            rows = pl.ds(pl.multiple_of(l * 1024 + base, 128), 128)
            scale = block_scale(expt[:, rows])
            scale = jnp.concatenate([scale, jnp.zeros((4, 128), F32)], axis=0)
            spread = lax.dot_general(scale, pick, (((0,), (0,)), ((), ())), preferred_element_type=F32)
            for k in range(4):
                cols = pl.ds(k * 128, 128)
                piece = (graw[p, l, :, cols].astype(F32) * spread[:, k * 128 : (k + 1) * 128]).astype(BF16)
                piece = piece.reshape(2, 4, 16, 128)
                for h in range(2):
                    dec[2 * p + flip(odd, h), l // 4, l % 4, pl.ds(4 * k, 4)] = piece[h]
            return 0

        lax.fori_loop(0, 8, one, 0)

    def first(t):
        for i in range(3):
            rs(t, i).start()

    def second(t):
        o = own(t)
        for i in range(3):
            rs(t, i).wait_recv()
        at = (t, slice(None), xp, pl.ds(0, XP))
        dec[at] = (wide(dec, *at) + wide(r1p, t)).astype(BF16)
        rs(t, 3).start()
        at = (t, slice(None), xm, pl.ds(XP, XT - XP))
        dec[at] = (wide(dec, *at) + wide(r1m, t)).astype(BF16)
        rs(t, 4).start()
        at = (t, o, slice(None), pl.ds(XT, YT))
        dec[at] = (wide(dec, *at) + wide(r1y, t)).astype(BF16)
        rs(t, 5).start()
        rs(t, 6).start()
        for i in range(3):
            rs(t, i).wait_send()

    def third(t):
        o = own(t)
        for i in range(3, 7):
            rs(t, i).wait_recv()
        at = (t, 1 - o, x, pl.ds(0, XT))
        dec[at] = (wide(dec, *at) + wide(r2p, t, 1 - o) + wide(r2m, t, 1 - o)).astype(BF16)
        rs(t, 7).start()
        at = (t, o, xp, pl.ds(XT, YP))
        dec[at] = (wide(dec, *at) + wide(q2p, t)).astype(BF16)
        rs(t, 8).start()
        at = (t, o, xm, pl.ds(YM, YT - YP))
        dec[at] = (wide(dec, *at) + wide(q2m, t)).astype(BF16)
        rs(t, 9).start()
        for i in range(3, 7):
            rs(t, i).wait_send()

    def fourth(t):
        o = own(t)
        for i in range(7, 10):
            rs(t, i).wait_recv()
        at = (t, o, x, pl.ds(0, XT))
        dec[at] = (wide(dec, *at) + wide(r2p, t, o) + wide(r2m, t, o) + wide(r3x, t)).astype(BF16)
        at = (t, o, x, pl.ds(XT, YT))
        dec[at] = (wide(dec, *at) + wide(q3p, t) + wide(q3m, t)).astype(BF16)

        @pl.when(t > 0)
        def _():
            go(t).start()

        @pl.when(t == 0)
        def _():
            a2a[0] = dec[0, yl, x]

        for i in range(7, 10):
            rs(t, i).wait_send()

    def fifth(t):
        for copy in load_m(t):
            copy.wait()

        @pl.when(t > 0)
        def _():
            go(t).wait_recv()

        for k in range(4):
            cols = pl.ds(k * 128, 128)
            average = wide(a2a, t, pl.ds(4 * k, 4)).reshape(64, 128) / F32(8)
            moved = outer_momentum * mom[t, :, cols] + average
            params = mas[t, :, cols] - outer_rate * (average + outer_momentum * moved)
            omom[t, :, cols] = moved
            omas[t, :, cols] = params
            ret[t, pl.ds(4 * k, 4)] = params.astype(BF16).reshape(4, 16, 128)

        @pl.when(t > 0)
        def _():
            back(t).start()
            go(t).wait_send()

        @pl.when(t == 0)
        def _():
            back_own().start()

        for copy in store_m(t):
            copy.start()

    def sixth(t):
        @pl.when(t > 0)
        def _():
            back(t, True).wait_recv()

        @pl.when(t == 0)
        def _():
            back_own().wait()

        for i in range(3):
            ag(t, i).start()

        @pl.when(t > 0)
        def _():
            back(t).wait_send()

    def seventh(t):
        for i in range(3):
            ag(t, i, True).wait_recv()
        for i in range(3, 7):
            ag(t, i).start()
        for i in range(3):
            ag(t, i).wait_send()

    def eighth(t):
        for i in range(3, 7):
            ag(t, i, True).wait_recv()
        for i in range(7, 10):
            ag(t, i).start()
        for i in range(3, 7):
            ag(t, i).wait_send()

    def ninth(t):
        for i in range(7, 10):
            ag(t, i, True).wait_recv()
        for i in range(7, 10):
            ag(t, i).wait_send()
        for copy in store_m(t):
            copy.wait()

    for p in range(UNITS // 2):
        load_g(p).start()

    barrier = pltpu.get_barrier_semaphore()
    friends = [right, left, side] + [partner(t) for t in range(1, UNITS)]
    for device in friends:
        pl.semaphore_signal(barrier, inc=1, device_id=device, device_id_type=MESH)

    def start_m(t, _):
        for copy in load_m(t):
            copy.start()
        return 0

    lax.fori_loop(0, UNITS, start_m, 0)
    decode(0)
    pl.semaphore_wait(barrier, len(friends))

    stages = (first, second, third, fourth, fifth, sixth, seventh, eighth, ninth)

    def step(s, _):
        for lag, stage in enumerate(stages):

            @pl.when((s >= lag) & (s < UNITS + lag))
            def _(lag=lag, stage=stage):
                stage(s - lag)

            if lag == 0:

                @pl.when((s % 2 == 1) & (s < UNITS - 1))
                def _():
                    decode((s + 1) // 2)

        return 0

    lax.fori_loop(0, UNITS + len(stages) - 1, step, 0)


def order_kernel(layout, raw, out):
    for j in range(UNITS):
        for k in range(4):
            out[pl.ds(j * 64, 64), pl.ds(k * 128, 128)] = raw[j, 0, 0, pl.ds(4 * k, 4)].reshape(64, 128)


def per_device(pseudo_grads, exponents, master, momentum, layout):
    tiles = (TILES, 16, 128)
    vmem = lambda *shape: pltpu.VMEM(shape + (16, 128), BF16)
    dma = lambda *shape: pltpu.SemaphoreType.DMA(shape)
    far = pl.BlockSpec(memory_space=pl.ANY)
    raw, new_master, new_momentum = pl.pallas_call(
        step_kernel,
        out_shape=(
            jax.ShapeDtypeStruct((UNITS, 2, 4) + tiles, BF16),
            jax.ShapeDtypeStruct(master.shape, F32),
            jax.ShapeDtypeStruct(master.shape, F32),
        ),
        in_specs=[far, pl.BlockSpec(memory_space=pltpu.VMEM), far, far],
        out_specs=(far, far, far),
        scratch_shapes=[
            pltpu.VMEM((UNITS // 2, 8, 128, 512), BF16),
            vmem(UNITS, 2, 4, TILES),
            vmem(UNITS, 2, XP),
            vmem(UNITS, 2, XT - XP),
            vmem(UNITS, 4, YT),
            vmem(UNITS, 2, XT),
            vmem(UNITS, 2, XT),
            vmem(UNITS, YP),
            vmem(UNITS, YT - YP),
            vmem(UNITS, XT),
            vmem(UNITS, YT),
            vmem(UNITS, YT),
            vmem(UNITS, TILES),
            vmem(UNITS, TILES),
        ]
        + [pltpu.VMEM((UNITS, 64, 512), F32)] * 4
        + [
            dma(UNITS // 2),
            dma(2, UNITS),
            dma(2, UNITS),
            pltpu.SemaphoreType.DMA,
            dma(UNITS, 10),
            dma(UNITS, 10),
            dma(UNITS),
            dma(UNITS),
            dma(UNITS),
            dma(UNITS),
            dma(UNITS, 10),
            dma(UNITS, 10),
        ],
        compiler_params=pltpu.CompilerParams(
            collective_id=0, has_side_effects=True, vmem_limit_bytes=56 * 2**20
        ),
        name="sum_update_gather",
    )(pseudo_grads.reshape(8, 8, 128, 512), exponents[0].T, master, momentum)

    island = pl.pallas_call(
        order_kernel,
        out_shape=jax.ShapeDtypeStruct((8192, 512), BF16),
        grid_spec=pltpu.PrefetchScalarGridSpec(
            num_scalar_prefetch=1,
            grid=(8,),
            in_specs=[
                pl.BlockSpec(
                    (UNITS, 1, 1) + tiles, lambda s, layout: (0, layout[s] // 4, layout[s] % 4, 0, 0, 0)
                )
            ],
            out_specs=pl.BlockSpec((1024, 512), lambda s, layout: (s, 0)),
        ),
        compiler_params=pltpu.CompilerParams(vmem_limit_bytes=32 * 2**20),
        name="layer_order",
    )(layout, raw)
    return new_master, new_momentum, island


def solution(mesh):
    rows = P(("replica", "fsdp"), None)
    grads = P("replica", None, "fsdp")
    return jax.shard_map(
        per_device,
        mesh=mesh,
        in_specs=(grads, grads, rows, rows, P()),
        out_specs=(rows, rows, P(None, "fsdp")),
        check_vma=False,
    )
```

```python
import jax
import jax.numpy as jnp
from jax import lax
from jax.experimental import pallas as pl
from jax.experimental.pallas import tpu as pltpu
from jax.sharding import PartitionSpec as P

MESH = pl.DeviceIdType.MESH
F32, BF16 = jnp.float32, jnp.bfloat16

outer_rate = 0.7
outer_momentum = 0.9

UNITS = 16
TILES = 16
XT = 9
XP = 5
YT = TILES - XT
YP = 3
YM = XT + YP
LAGS = (0, 3, 6, 9, 12, 15, 18, 21, 24)


def bit(v, b):
    return (v // (1 << b)) % 2


def flip(a, b):
    return a + b - 2 * a * b


def xor16(f, t):
    return sum(flip(bit(f, b), bit(t, b)) * (1 << b) for b in range(4))


def block_scale(exponents):
    scale = jnp.zeros(exponents.shape, F32)
    for level in range(-6, 2):
        scale = jnp.where(exponents == level, F32(2.0**level), scale)
    return scale


def step_kernel(
    g, expt, master, momentum,
    isl, new_master, new_momentum,
    graw, dec, r1p, r1m, r1y, r2p, r2m, q2p, q2m, r3x, q3p, q3m, a2a, ret, mas, mom, omas, omom,
    g_sem, m_sem, o_sem, own_sem, rs_send, rs_recv, a_send, a_recv, b_send, b_recv, ag_send, ag_recv,
):
    rep, fs = lax.axis_index("replica"), lax.axis_index("fsdp")
    x, yl = rep % 4, rep // 4
    turn = 2 * (fs % 2)
    xp, xm, xo = (x + 1 + turn) % 4, (x + 3 + turn) % 4, (x + 2) % 4
    right, left, side = (yl * 4 + xp, fs), (yl * 4 + xm, fs), ((1 - yl) * 4 + x, fs)

    def own(t):
        return flip(yl, bit(t, 1))

    def partner(t):
        return (own(t) * 4 + x, xor16(fs, t))

    def columns(t):
        return pl.ds(pl.multiple_of(xor16(fs, t) * 512, 512), 512)

    def load_g(p):
        return pltpu.make_async_copy(g.at[:, xor16(fs, 2 * p) // 2], graw.at[p], g_sem.at[p])

    def load_m(t):
        return (
            pltpu.make_async_copy(master.at[:, columns(t)], mas.at[t], m_sem.at[0, t]),
            pltpu.make_async_copy(momentum.at[:, columns(t)], mom.at[t], m_sem.at[1, t]),
        )

    def store_m(t):
        return (
            pltpu.make_async_copy(omas.at[t], new_master.at[xor16(fs, t)], o_sem.at[0, t]),
            pltpu.make_async_copy(omom.at[t], new_momentum.at[xor16(fs, t)], o_sem.at[1, t]),
        )

    def remote(src, dst, send, recv, device):
        return pltpu.make_async_remote_copy(
            src_ref=src, dst_ref=dst, send_sem=send, recv_sem=recv, device_id=device, device_id_type=MESH
        )

    def rs(t, i):
        o = own(t)
        every = slice(None)
        src, dst, device = (
            (dec.at[t, every, xo, pl.ds(0, XP)], r1p, right),
            (dec.at[t, every, xo, pl.ds(XP, XT - XP)], r1m, left),
            (dec.at[t, 1 - o, every, pl.ds(XT, YT)], r1y, side),
            (dec.at[t, every, xp, pl.ds(0, XT)], r2p, right),
            (dec.at[t, every, xm, pl.ds(0, XT)], r2m, left),
            (dec.at[t, o, xo, pl.ds(XT, YP)], q2p, right),
            (dec.at[t, o, xo, pl.ds(YM, YT - YP)], q2m, left),
            (dec.at[t, 1 - o, x, pl.ds(0, XT)], r3x, side),
            (dec.at[t, o, xp, pl.ds(XT, YT)], q3p, right),
            (dec.at[t, o, xm, pl.ds(XT, YT)], q3m, left),
        )[i]
        return remote(src, dst.at[t], rs_send.at[t, i], rs_recv.at[t, i], device)

    def ag(t, i, arriving=False):
        o, j = own(t), xor16(fs, t)
        every = slice(None)
        cp, cm = (xm, xp) if arriving else (x, x)
        fp, fm = (xo, xo) if arriving else (xm, xp)
        mine = 1 - o if arriving else o
        ref, device = (
            (isl.at[j, mine, x, pl.ds(0, XT)], side),
            (isl.at[j, o, cp, pl.ds(XT, YT)], right),
            (isl.at[j, o, cm, pl.ds(XT, YT)], left),
            (isl.at[j, every, cp, pl.ds(0, XT)], right),
            (isl.at[j, every, cm, pl.ds(0, XT)], left),
            (isl.at[j, o, fp, pl.ds(XT, YP)], right),
            (isl.at[j, o, fm, pl.ds(YM, YT - YP)], left),
            (isl.at[j, every, fp, pl.ds(0, XP)], right),
            (isl.at[j, every, fm, pl.ds(XP, XT - XP)], left),
            (isl.at[j, mine, every, pl.ds(XT, YT)], side),
        )[i]
        return remote(ref, ref, ag_send.at[t, i], ag_recv.at[t, i], device)

    def go(t):
        return remote(dec.at[t, own(t), x], a2a.at[t], a_send.at[t], a_recv.at[t], partner(t))

    def back(t, arriving=False):
        place = isl.at[xor16(fs, t), own(t), x] if arriving else isl.at[fs, yl, x]
        return remote(ret.at[t], place, b_send.at[t], b_recv.at[t], partner(t))

    def back_own():
        return pltpu.make_async_copy(ret.at[0], isl.at[fs, yl, x], own_sem)

    def wide(ref, *at):
        return ref[at].astype(F32)

    lane_block = lax.broadcasted_iota(jnp.int32, (8, 512), 1) // 128
    pick = (lane_block == lax.broadcasted_iota(jnp.int32, (8, 512), 0)).astype(F32)

    def decode(p):
        load_g(p).wait()
        base = xor16(fs, 2 * p) // 2 * 128
        odd = fs % 2

        def one(l, _):
            rows = pl.ds(pl.multiple_of(l * 1024 + base, 128), 128)
            scale = block_scale(expt[:, rows])
            scale = jnp.concatenate([scale, jnp.zeros((4, 128), F32)], axis=0)
            spread = lax.dot_general(scale, pick, (((0,), (0,)), ((), ())), preferred_element_type=F32).astype(BF16)
            for k in range(4):
                cols = pl.ds(k * 128, 128)
                piece = graw[p, l, :, cols] * spread[:, k * 128 : (k + 1) * 128]
                piece = piece.reshape(2, 4, 16, 128)
                for h in range(2):
                    dec[2 * p + flip(odd, h), l // 4, l % 4, pl.ds(4 * k, 4)] = piece[h]
            return 0

        lax.fori_loop(0, 8, one, 0)

    def first(t):
        for i in range(3):
            rs(t, i).start()

    def second(t):
        o = own(t)
        for i in range(3):
            rs(t, i).wait_recv()
        at = (t, slice(None), xp, pl.ds(0, XP))
        dec[at] = (wide(dec, *at) + wide(r1p, t)).astype(BF16)
        rs(t, 3).start()
        at = (t, slice(None), xm, pl.ds(XP, XT - XP))
        dec[at] = (wide(dec, *at) + wide(r1m, t)).astype(BF16)
        rs(t, 4).start()
        at = (t, o, slice(None), pl.ds(XT, YT))
        dec[at] = (wide(dec, *at) + wide(r1y, t)).astype(BF16)
        rs(t, 5).start()
        rs(t, 6).start()
        for i in range(3):
            rs(t, i).wait_send()

    def third(t):
        o = own(t)
        for i in range(3, 7):
            rs(t, i).wait_recv()
        at = (t, 1 - o, x, pl.ds(0, XT))
        dec[at] = (wide(dec, *at) + wide(r2p, t, 1 - o) + wide(r2m, t, 1 - o)).astype(BF16)
        rs(t, 7).start()
        at = (t, o, xp, pl.ds(XT, YP))
        dec[at] = (wide(dec, *at) + wide(q2p, t)).astype(BF16)
        rs(t, 8).start()
        at = (t, o, xm, pl.ds(YM, YT - YP))
        dec[at] = (wide(dec, *at) + wide(q2m, t)).astype(BF16)
        rs(t, 9).start()
        for i in range(3, 7):
            rs(t, i).wait_send()

    def fourth(t):
        o = own(t)
        for i in range(7, 10):
            rs(t, i).wait_recv()
        at = (t, o, x, pl.ds(0, XT))
        dec[at] = (wide(dec, *at) + wide(r2p, t, o) + wide(r2m, t, o) + wide(r3x, t)).astype(BF16)
        at = (t, o, x, pl.ds(XT, YT))
        dec[at] = (wide(dec, *at) + wide(q3p, t) + wide(q3m, t)).astype(BF16)

        @pl.when(t > 0)
        def _():
            go(t).start()

        @pl.when(t == 0)
        def _():
            a2a[0] = dec[0, yl, x]

        for i in range(7, 10):
            rs(t, i).wait_send()

    def fifth(t):
        for copy in load_m(t):
            copy.wait()

        @pl.when(t > 0)
        def _():
            go(t).wait_recv()

        for k in range(4):
            cols = pl.ds(k * 128, 128)
            average = wide(a2a, t, pl.ds(4 * k, 4)).reshape(64, 128) / F32(8)
            moved = outer_momentum * mom[t, :, cols] + average
            params = mas[t, :, cols] - outer_rate * (average + outer_momentum * moved)
            omom[t, :, cols] = moved
            omas[t, :, cols] = params
            ret[t, pl.ds(4 * k, 4)] = params.astype(BF16).reshape(4, 16, 128)

        @pl.when(t > 0)
        def _():
            back(t).start()
            go(t).wait_send()

        @pl.when(t == 0)
        def _():
            back_own().start()

        for copy in store_m(t):
            copy.start()

    def sixth(t):
        @pl.when(t > 0)
        def _():
            back(t, True).wait_recv()

        @pl.when(t == 0)
        def _():
            back_own().wait()

        for i in range(3):
            ag(t, i).start()

        @pl.when(t > 0)
        def _():
            back(t).wait_send()

    def seventh(t):
        for i in range(3):
            ag(t, i, True).wait_recv()
        for i in range(3, 7):
            ag(t, i).start()
        for i in range(3):
            ag(t, i).wait_send()

    def eighth(t):
        for i in range(3, 7):
            ag(t, i, True).wait_recv()
        for i in range(7, 10):
            ag(t, i).start()
        for i in range(3, 7):
            ag(t, i).wait_send()

    def ninth(t):
        for i in range(7, 10):
            ag(t, i, True).wait_recv()
        for i in range(7, 10):
            ag(t, i).wait_send()
        for copy in store_m(t):
            copy.wait()

    for p in range(UNITS // 2):
        load_g(p).start()

    barrier = pltpu.get_barrier_semaphore()
    friends = [right, left, side] + [partner(t) for t in range(1, UNITS)]
    for device in friends:
        pl.semaphore_signal(barrier, inc=1, device_id=device, device_id_type=MESH)

    def start_m(t, _):
        for copy in load_m(t):
            copy.start()
        return 0

    lax.fori_loop(0, UNITS, start_m, 0)
    decode(0)
    pl.semaphore_wait(barrier, len(friends))

    stages = (first, second, third, fourth, fifth, sixth, seventh, eighth, ninth)

    def step(s, _):
        for lag, stage in zip(LAGS, stages):

            @pl.when((s >= lag) & (s < UNITS + lag))
            def _(lag=lag, stage=stage):
                stage(s - lag)

            if lag == 0:

                @pl.when((s % 2 == 1) & (s < UNITS - 1))
                def _():
                    decode((s + 1) // 2)

        return 0

    lax.fori_loop(0, UNITS + LAGS[-1], step, 0)


def order_kernel(layout, raw, mas, mom, out, new_master, new_momentum, staged, sems, more_sems):
    copies = []
    for f in range(UNITS):
        for i, (ref, to) in enumerate(((mas, new_master), (mom, new_momentum))):
            copies.append(pltpu.make_async_copy(ref.at[f], to.at[:, pl.ds(f * 512, 512)], more_sems.at[i, f]))
            copies[-1].start()
    for s in range(8):
        l = layout[s]

        def one(j, _, s=s, l=l):
            rows = pl.ds(pl.multiple_of(j * 64, 64), 64)
            for k in range(4):
                staged[s, rows, pl.ds(128 * k, 128)] = raw[j, l // 4, l % 4, pl.ds(4 * k, 4)].reshape(64, 128)
            return 0

        lax.fori_loop(0, UNITS, one, 0)
        copies.append(pltpu.make_async_copy(staged.at[s], out.at[pl.ds(s * 1024, 1024)], sems.at[s]))
        copies[-1].start()
    for copy in copies:
        copy.wait()


def per_device(pseudo_grads, exponents, master, momentum, layout):
    tiles = (TILES, 16, 128)
    vmem = lambda *shape: pltpu.VMEM(shape + (16, 128), BF16)
    dma = lambda *shape: pltpu.SemaphoreType.DMA(shape)
    far = pl.BlockSpec(memory_space=pl.ANY)
    results = pl.pallas_call(
        step_kernel,
        out_shape=(
            pltpu.VMEM((UNITS, 2, 4) + tiles, BF16),
            pltpu.VMEM((UNITS, 64, 512), F32),
            pltpu.VMEM((UNITS, 64, 512), F32),
        ),
        in_specs=[far, pl.BlockSpec(memory_space=pltpu.VMEM), far, far],
        out_specs=(far, far, far),
        scratch_shapes=[
            pltpu.VMEM((UNITS // 2, 8, 128, 512), BF16),
            vmem(UNITS, 2, 4, TILES),
            vmem(UNITS, 2, XP),
            vmem(UNITS, 2, XT - XP),
            vmem(UNITS, 4, YT),
            vmem(UNITS, 2, XT),
            vmem(UNITS, 2, XT),
            vmem(UNITS, YP),
            vmem(UNITS, YT - YP),
            vmem(UNITS, XT),
            vmem(UNITS, YT),
            vmem(UNITS, YT),
            vmem(UNITS, TILES),
            vmem(UNITS, TILES),
        ]
        + [pltpu.VMEM((UNITS, 64, 512), F32)] * 4
        + [
            dma(UNITS // 2),
            dma(2, UNITS),
            dma(2, UNITS),
            pltpu.SemaphoreType.DMA,
            dma(UNITS, 10),
            dma(UNITS, 10),
            dma(UNITS),
            dma(UNITS),
            dma(UNITS),
            dma(UNITS),
            dma(UNITS, 10),
            dma(UNITS, 10),
        ],
        compiler_params=pltpu.CompilerParams(
            collective_id=0, has_side_effects=True, vmem_limit_bytes=48 * 2**20
        ),
        name="sum_update_gather",
    )(pseudo_grads.reshape(8, 8, 128, 512), exponents[0].T, master, momentum)

    near = pl.BlockSpec(memory_space=pltpu.VMEM)
    island, new_master, new_momentum = pl.pallas_call(
        order_kernel,
        out_shape=(
            jax.ShapeDtypeStruct((8192, 512), BF16),
            jax.ShapeDtypeStruct(master.shape, F32),
            jax.ShapeDtypeStruct(master.shape, F32),
        ),
        in_specs=[pl.BlockSpec(memory_space=pltpu.SMEM), near, near, near],
        out_specs=(far, far, far),
        scratch_shapes=[pltpu.VMEM((8, 1024, 512), BF16), dma(8), dma(2, UNITS)],
        compiler_params=pltpu.CompilerParams(vmem_limit_bytes=12 * 2**20),
        name="layer_order",
    )(layout, *results)
    return new_master, new_momentum, island


def solution(mesh):
    rows = P(("replica", "fsdp"), None)
    grads = P("replica", None, "fsdp")
    return jax.shard_map(
        per_device,
        mesh=mesh,
        in_specs=(grads, grads, rows, rows, P()),
        out_specs=(rows, rows, P(None, "fsdp")),
        check_vma=False,
    )
```

```python
import jax
import jax.numpy as jnp
from jax import lax
from jax.experimental import pallas as pl
from jax.experimental.pallas import tpu as pltpu
from jax.sharding import PartitionSpec as P

MESH = pl.DeviceIdType.MESH
F32, BF16 = jnp.float32, jnp.bfloat16

outer_rate = 0.7
outer_momentum = 0.9

UNITS = 16
TILES = 16
XT = 9
XP = 5
YT = TILES - XT
YP = 3
YM = XT + YP


ORDER = (
    ("x1", 0), ("y1", 0), ("decode", 0), ("x2", 3), ("y2", 3), ("x3", 6), ("y3", 6), ("z4", 9), ("z5", 12),
    ("gx1", 15), ("gy1", 15), ("gx2", 18), ("gy2", 18), ("gx3", 21), ("gy3", 21),
)


def bit(v, b):
    return lax.rem(lax.div(v, 1 << b), 2)


def flip(a, b):
    return a + b - 2 * a * b


def block_scale(exponents):
    scale = jnp.zeros(exponents.shape, F32)
    for level in range(-6, 2):
        scale = jnp.where(exponents == level, F32(2.0**level), scale)
    return scale


def step_kernel(
    g, expt, master, momentum,
    isl, new_master, new_momentum,
    graw, dec, r1x, r1y, r2x, r2y, r3, a2a, ret, mas, mom,
    g_sem, m_sem, own_sem, send_sem, x1_sem, y1_sem, x2_sem, y2_sem, r3_sem, a_sem, b_sem,
    gx1_sem, gy1_sem, gx2_sem, gy2_sem, gx3_sem, gy3_sem,
):
    rep, fs = lax.axis_index("replica"), lax.axis_index("fsdp")
    x, yl = lax.rem(rep, 4), lax.div(rep, 4)
    turn = 2 * lax.rem(fs, 2)
    xp, xm, xo = lax.rem(x + 1 + turn, 4), lax.rem(x + 3 + turn, 4), lax.rem(x + 2, 4)
    right, left, side = (yl * 4 + xp, fs), (yl * 4 + xm, fs), ((1 - yl) * 4 + x, fs)
    swaps = [(1 - 2 * bit(fs, b)) * (1 << b) for b in range(4)]
    every = slice(None)
    tx, ty = pl.ds(0, XT), pl.ds(XT, YT)
    txp, txm = pl.ds(0, XP), pl.ds(XP, XT - XP)
    typ, tym = pl.ds(XT, YP), pl.ds(YM, YT - YP)

    def other(t):
        return fs + sum(bit(t, b) * swaps[b] for b in range(4))

    def own(t):
        return flip(yl, bit(t, 1))

    def partner(t):
        return (own(t) * 4 + x, other(t))

    def columns(t):
        return pl.ds(pl.multiple_of(other(t) * 512, 512), 512)

    def load_g(p):
        return pltpu.make_async_copy(g.at[:, lax.div(other(2 * p), 2)], graw.at[p], g_sem.at[p])

    loads = (
        pltpu.make_async_copy(master, mas, m_sem.at[0]),
        pltpu.make_async_copy(momentum, mom, m_sem.at[1]),
    )

    def remote(src, dst, send, recv, device):
        return pltpu.make_async_remote_copy(
            src_ref=src, dst_ref=dst, send_sem=send_sem.at[send], recv_sem=recv, device_id=device, device_id_type=MESH
        )

    def send(src, dst, recv, device):
        remote(src, dst, 0, recv, device).start()

    def spread(ref, recv, device):
        remote(ref, ref, 1, recv, device).start()

    def arrived(ref, recv):
        remote(ref, ref, 0, recv, right).wait_recv()

    def wide(ref, *at):
        return ref[at].astype(F32)

    def z4_copy(t):
        return remote(dec.at[t, own(t), x], a2a.at[t], 2, a_sem.at[t], partner(t))

    def z5_copy(t):
        return remote(ret.at[t], isl.at[fs, yl, x], 3, b_sem.at[t], partner(t))

    def z5_own():
        return pltpu.make_async_copy(ret.at[0], isl.at[fs, yl, x], own_sem)

    lane_block = lax.broadcasted_iota(jnp.int32, (8, 512), 1) // 128
    pick = (lane_block == lax.broadcasted_iota(jnp.int32, (8, 512), 0)).astype(F32)

    def decode(p):
        load_g(p).wait()
        base = lax.div(other(2 * p), 2) * 128
        odd = lax.rem(fs, 2)

        def one(l, _):
            rows = pl.ds(pl.multiple_of(l * 1024 + base, 128), 128)
            scale = block_scale(expt[:, rows])
            scale = jnp.concatenate([scale, jnp.zeros((4, 128), F32)], axis=0)
            scales = lax.dot_general(scale, pick, (((0,), (0,)), ((), ())), preferred_element_type=F32).astype(BF16)
            for k in range(4):
                piece = graw[p, l, :, pl.ds(k * 128, 128)] * scales[:, k * 128 : (k + 1) * 128]
                piece = piece.reshape(2, 4, 16, 128)
                for h in range(2):
                    dec[2 * p + flip(odd, h), lax.div(l, 4), lax.rem(l, 4), pl.ds(4 * k, 4)] = piece[h]
            return 0

        lax.fori_loop(0, 8, one, 0)

    def x1(t):
        send(dec.at[t, every, xo, txp], r1x.at[t, every, txp], x1_sem.at[t], right)
        send(dec.at[t, every, xo, txm], r1x.at[t, every, txm], x1_sem.at[t], left)

    def y1(t):
        send(dec.at[t, 1 - own(t), every, ty], r1y.at[t], y1_sem.at[t], side)

    def x2(t):
        arrived(r1x.at[t], x1_sem.at[t])
        at = (t, every, xp, txp)
        dec[at] = (wide(dec, *at) + wide(r1x, t, every, txp)).astype(BF16)
        send(dec.at[t, every, xp, tx], r2x.at[t, 0], x2_sem.at[t], right)
        at = (t, every, xm, txm)
        dec[at] = (wide(dec, *at) + wide(r1x, t, every, txm)).astype(BF16)
        send(dec.at[t, every, xm, tx], r2x.at[t, 1], x2_sem.at[t], left)

    def y2(t):
        arrived(r1y.at[t], y1_sem.at[t])
        o = own(t)
        at = (t, o, every, ty)
        dec[at] = (wide(dec, *at) + wide(r1y, t)).astype(BF16)
        send(dec.at[t, o, xo, typ], r2y.at[t, pl.ds(0, YP)], y2_sem.at[t], right)
        send(dec.at[t, o, xo, tym], r2y.at[t, pl.ds(YP, YT - YP)], y2_sem.at[t], left)

    def x3(t):
        arrived(r2x.at[t], x2_sem.at[t])
        o = 1 - own(t)
        at = (t, o, x, tx)
        dec[at] = (wide(dec, *at) + wide(r2x, t, 0, o) + wide(r2x, t, 1, o)).astype(BF16)
        send(dec.at[at], r3.at[t, tx], r3_sem.at[t], side)

    def y3(t):
        arrived(r2y.at[t], y2_sem.at[t])
        o = own(t)
        at = (t, o, xp, typ)
        dec[at] = (wide(dec, *at) + wide(r2y, t, pl.ds(0, YP))).astype(BF16)
        send(dec.at[t, o, xp, ty], r3.at[t, pl.ds(XT, YT)], r3_sem.at[t], right)
        at = (t, o, xm, tym)
        dec[at] = (wide(dec, *at) + wide(r2y, t, pl.ds(YP, YT - YP))).astype(BF16)
        send(dec.at[t, o, xm, ty], r3.at[t, pl.ds(XT + YT, YT)], r3_sem.at[t], left)

    def z4(t):
        arrived(r3.at[t], r3_sem.at[t])
        o = own(t)
        at = (t, o, x, tx)
        dec[at] = (wide(dec, *at) + wide(r2x, t, 0, o) + wide(r2x, t, 1, o) + wide(r3, t, tx)).astype(BF16)
        at = (t, o, x, ty)
        dec[at] = (wide(dec, *at) + wide(r3, t, ty) + wide(r3, t, pl.ds(XT + YT, YT))).astype(BF16)

        @pl.when(t > 0)
        def _():
            z4_copy(t).start()

        @pl.when(t == 0)
        def _():
            a2a[0] = dec[0, yl, x]

    def z5(t):
        @pl.when(t > 0)
        def _():
            z4_copy(t).wait_recv()

        @pl.when(t == 0)
        def _():
            for load in loads:
                load.wait()

        for k in range(4):
            cols = pl.ds(pl.multiple_of(other(t) * 512 + k * 128, 128), 128)
            average = wide(a2a, t, pl.ds(4 * k, 4)).reshape(64, 128) / F32(8)
            moved = outer_momentum * mom[:, cols] + average
            params = mas[:, cols] - outer_rate * (average + outer_momentum * moved)
            new_momentum[:, cols] = moved
            new_master[:, cols] = params
            ret[t, pl.ds(4 * k, 4)] = params.astype(BF16).reshape(4, 16, 128)

        @pl.when(t > 0)
        def _():
            z5_copy(t).start()

        @pl.when(t == 0)
        def _():
            z5_own().start()

    def ready(t):
        @pl.when(t > 0)
        def _():
            arrived(isl.at[other(t), own(t), x], b_sem.at[t])

        @pl.when(t == 0)
        def _():
            z5_own().wait()

    def gx1(t):
        ready(t)
        spread(isl.at[other(t), own(t), x, tx], gx1_sem.at[t], side)

    def gy1(t):
        at = isl.at[other(t), own(t), x, ty]
        spread(at, gy1_sem.at[t], right)
        spread(at, gy1_sem.at[t], left)

    def gx2(t):
        j = other(t)
        arrived(isl.at[j, 1 - own(t), x, tx], gx1_sem.at[t])
        at = isl.at[j, every, x, tx]
        spread(at, gx2_sem.at[t], right)
        spread(at, gx2_sem.at[t], left)

    def gy2(t):
        j, o = other(t), own(t)
        arrived(isl.at[j, every, x, ty], gy1_sem.at[t])
        spread(isl.at[j, o, xm, typ], gy2_sem.at[t], right)
        spread(isl.at[j, o, xp, tym], gy2_sem.at[t], left)

    def gx3(t):
        j = other(t)
        arrived(isl.at[j, every, pl.ds(0, 2), tx], gx2_sem.at[t])
        spread(isl.at[j, every, xm, txp], gx3_sem, right)
        spread(isl.at[j, every, xp, txm], gx3_sem, left)

    def gy3(t):
        j, o = other(t), own(t)
        arrived(isl.at[j, o, xo, ty], gy2_sem.at[t])
        spread(isl.at[j, o, every, ty], gy3_sem, side)

    barrier = pltpu.get_barrier_semaphore()
    load_g(0).start()
    friends = [right, left, side] + [partner(jnp.int32(t)) for t in range(1, UNITS)]
    for device in friends:
        pl.semaphore_signal(barrier, inc=1, device_id=device, device_id_type=MESH)
    load_g(1).start()
    decode(0)
    for p in range(2, UNITS // 2):
        load_g(p).start()
    for load in loads:
        load.start()
    pl.semaphore_wait(barrier, len(friends))

    stages = dict(
        x1=x1, y1=y1, x2=x2, y2=y2, x3=x3, y3=y3, z4=z4, z5=z5, gx1=gx1, gy1=gy1, gx2=gx2, gy2=gy2, gx3=gx3, gy3=gy3
    )

    def step(s, _):
        for name, lag in ORDER:
            if name == "decode":

                @pl.when((lax.rem(s, 2) == 1) & (s < UNITS - 1))
                def _():
                    decode(lax.div(s + 1, 2))

            else:

                @pl.when((s >= lag) & (s < UNITS + lag))
                def _(lag=lag, stage=stages[name]):
                    stage(s - lag)

        return 0

    lax.fori_loop(0, UNITS + max(lag for _, lag in ORDER), step, 0)

    arrived(isl.at[every, every, xo, tx], gx3_sem)
    arrived(isl.at[every, 0, every, ty], gy3_sem)
    for i, ref in enumerate(
        (dec.at[every, every, every, pl.ds(0, 14)], isl.at[every, every, every, pl.ds(0, 14)], a2a.at[pl.ds(1, 15)], ret.at[pl.ds(1, 15)])
    ):
        remote(ref, ref, i, gx3_sem, right).wait_send()


def order_kernel(layout, raw, mas, mom, out, new_master, new_momentum, staged, sems):
    copies = [pltpu.make_async_copy(mas, new_master, sems.at[8]), pltpu.make_async_copy(mom, new_momentum, sems.at[9])]
    for copy in copies:
        copy.start()
    for s in range(8):
        l = layout[s]

        def one(j, _, s=s, l=l):
            rows = pl.ds(pl.multiple_of(j * 64, 64), 64)
            for k in range(4):
                staged[s, rows, pl.ds(128 * k, 128)] = raw[j, l // 4, l % 4, pl.ds(4 * k, 4)].reshape(64, 128)
            return 0

        lax.fori_loop(0, UNITS, one, 0)
        copies.append(pltpu.make_async_copy(staged.at[s], out.at[pl.ds(s * 1024, 1024)], sems.at[s]))
        copies[-1].start()
    for copy in copies:
        copy.wait()


def per_device(pseudo_grads, exponents, master, momentum, layout):
    tiles = (TILES, 16, 128)
    vmem = lambda *shape: pltpu.VMEM(shape + (16, 128), BF16)
    dma = lambda *shape: pltpu.SemaphoreType.DMA(shape)
    far = pl.BlockSpec(memory_space=pl.ANY)
    near = pl.BlockSpec(memory_space=pltpu.VMEM)
    results = pl.pallas_call(
        step_kernel,
        out_shape=(
            pltpu.VMEM((UNITS, 2, 4) + tiles, BF16),
            pltpu.VMEM(master.shape, F32),
            pltpu.VMEM(master.shape, F32),
        ),
        in_specs=[far, near, far, far],
        out_specs=(far, near, near),
        scratch_shapes=[
            pltpu.VMEM((UNITS // 2, 8, 128, 512), BF16),
            vmem(UNITS, 2, 4, TILES),
            vmem(UNITS, 2, XT),
            vmem(UNITS, 4, YT),
            vmem(UNITS, 2, 2, XT),
            vmem(UNITS, YT),
            vmem(UNITS, XT + 2 * YT),
            vmem(UNITS, TILES),
            vmem(UNITS, TILES),
            pltpu.VMEM(master.shape, F32),
            pltpu.VMEM(master.shape, F32),
            dma(UNITS // 2),
            dma(2),
            pltpu.SemaphoreType.DMA,
            dma(4),
        ]
        + [dma(UNITS)] * 11
        + [pltpu.SemaphoreType.DMA] * 2,
        compiler_params=pltpu.CompilerParams(
            collective_id=0, has_side_effects=True, vmem_limit_bytes=48 * 2**20
        ),
        name="sum_update_gather",
    )(pseudo_grads.reshape(8, 8, 128, 512), exponents[0].T, master, momentum)

    island, new_master, new_momentum = pl.pallas_call(
        order_kernel,
        out_shape=(
            jax.ShapeDtypeStruct((8192, 512), BF16),
            jax.ShapeDtypeStruct(master.shape, F32),
            jax.ShapeDtypeStruct(master.shape, F32),
        ),
        in_specs=[pl.BlockSpec(memory_space=pltpu.SMEM), near, near, near],
        out_specs=(far, far, far),
        scratch_shapes=[pltpu.VMEM((8, 1024, 512), BF16), dma(10)],
        compiler_params=pltpu.CompilerParams(vmem_limit_bytes=12 * 2**20),
        name="layer_order",
    )(layout, *results)
    return new_master, new_momentum, island


def solution(mesh):
    rows = P(("replica", "fsdp"), None)
    grads = P("replica", None, "fsdp")
    return jax.shard_map(
        per_device,
        mesh=mesh,
        in_specs=(grads, grads, rows, rows, P()),
        out_specs=(rows, rows, P(None, "fsdp")),
        check_vma=False,
    )
```

```python
import jax
import jax.numpy as jnp
from jax import lax
from jax.experimental import pallas as pl
from jax.experimental.pallas import tpu as pltpu
from jax.sharding import PartitionSpec as P

MESH = pl.DeviceIdType.MESH
F32, BF16 = jnp.float32, jnp.bfloat16

outer_rate = 0.7
outer_momentum = 0.9

UNITS = 16
TILES = 16
XT = 9
XP = 5
YT = TILES - XT
YP = 3
YM = XT + YP


ORDER = (
    ("x1", 0), ("y1", 0), ("decode", 0), ("x2", 3), ("y2", 4), ("x3", 6), ("y3", 6), ("z4", 9), ("z5", 11), ("gx1", 13), ("gy1", 13), ("gx2", 16), ("gy2", 15), ("gx3", 22), ("gy3", 17),
)


def bit(v, b):
    return lax.rem(lax.div(v, 1 << b), 2)


def flip(a, b):
    return a + b - 2 * a * b


def block_scale(exponents):
    scale = jnp.zeros(exponents.shape, F32)
    for level in range(-6, 2):
        scale = jnp.where(exponents == level, F32(2.0**level), scale)
    return scale


def step_kernel(
    g, exps, master, momentum,
    isl, new_master, new_momentum,
    graw, expt, dec, r1x, r1y, r2x, r2y, r3, a2a, ret, mas, mom,
    g_sem, e_sem, m_sem, own_sem, send_sem, x1_sem, y1_sem, x2_sem, y2_sem, r3_sem, a_sem, b_sem,
    gx1_sem, gy1_sem, gx2_sem, gy2_sem, gx3_sem, gy3_sem,
):
    rep, fs = lax.axis_index("replica"), lax.axis_index("fsdp")
    x, yl = lax.rem(rep, 4), lax.div(rep, 4)
    turn = 2 * lax.rem(fs, 2)
    xp, xm, xo = lax.rem(x + 1 + turn, 4), lax.rem(x + 3 + turn, 4), lax.rem(x + 2, 4)
    right, left, side = (yl * 4 + xp, fs), (yl * 4 + xm, fs), ((1 - yl) * 4 + x, fs)
    swaps = [(1 - 2 * bit(fs, b)) * (1 << b) for b in range(4)]
    every = slice(None)
    tx, ty = pl.ds(0, XT), pl.ds(XT, YT)
    txp, txm = pl.ds(0, XP), pl.ds(XP, XT - XP)
    typ, tym = pl.ds(XT, YP), pl.ds(YM, YT - YP)

    def other(t):
        return fs + sum(bit(t, b) * swaps[b] for b in range(4))

    def own(t):
        return flip(yl, bit(t, 1))

    def partner(t):
        return (own(t) * 4 + x, other(t))

    def columns(t):
        return pl.ds(pl.multiple_of(other(t) * 512, 512), 512)

    def load_g(p):
        return pltpu.make_async_copy(g.at[:, lax.div(other(2 * p), 2)], graw.at[p], g_sem.at[p])

    def load_half(h, sem):
        at = pl.ds(4 * h, 4)
        return pltpu.make_async_copy(g.at[at, lax.div(fs, 2)], graw.at[0, at], g_sem.at[sem])

    load_e = pltpu.make_async_copy(exps, expt, e_sem)
    loads = (
        pltpu.make_async_copy(master, mas, m_sem.at[0]),
        pltpu.make_async_copy(momentum, mom, m_sem.at[1]),
    )

    def remote(src, dst, send, recv, device):
        return pltpu.make_async_remote_copy(
            src_ref=src, dst_ref=dst, send_sem=send_sem.at[send], recv_sem=recv, device_id=device, device_id_type=MESH
        )

    def send(src, dst, recv, device):
        remote(src, dst, 0, recv, device).start()

    def spread(ref, recv, device):
        remote(ref, ref, 1, recv, device).start()

    def arrived(ref, recv):
        remote(ref, ref, 0, recv, right).wait_recv()

    def wide(ref, *at):
        return ref[at].astype(F32)

    def z4_copy(t):
        return remote(dec.at[t, own(t), x], a2a.at[t], 2, a_sem.at[t], partner(t))

    def z5_copy(t):
        return remote(ret.at[t], isl.at[fs, yl, x], 3, b_sem.at[t], partner(t))

    def z5_own():
        return pltpu.make_async_copy(ret.at[0], isl.at[fs, yl, x], own_sem)

    lane_block = lax.broadcasted_iota(jnp.int32, (8, 512), 1) // 128
    pick = (lane_block == lax.broadcasted_iota(jnp.int32, (8, 512), 0)).astype(F32)

    def decode_half(p, y):
        base = lax.div(other(2 * p), 2) * 128
        odd = lax.rem(fs, 2)
        for i in range(4):
            rows = pl.ds(pl.multiple_of((4 * y + i) * 1024 + base, 128), 128)
            scale = block_scale(expt[:, rows])
            scale = jnp.concatenate([scale, jnp.zeros((4, 128), F32)], axis=0)
            scales = lax.dot_general(scale, pick, (((0,), (0,)), ((), ())), preferred_element_type=F32).astype(BF16)
            for k in range(4):
                piece = graw[p, 4 * y + i, :, pl.ds(k * 128, 128)] * scales[:, k * 128 : (k + 1) * 128]
                piece = piece.reshape(2, 4, 16, 128)
                for h in range(2):
                    dec[2 * p + flip(odd, h), y, i, pl.ds(4 * k, 4)] = piece[h]

    def decode(p):
        load_g(p).wait()

        def one(y, _):
            decode_half(p, y)
            return 0

        lax.fori_loop(0, 2, one, 0)

    def x1(t):
        send(dec.at[t, every, xo, txp], r1x.at[t, every, txp], x1_sem.at[t], right)
        send(dec.at[t, every, xo, txm], r1x.at[t, every, txm], x1_sem.at[t], left)

    def y1(t):
        send(dec.at[t, 1 - own(t), every, ty], r1y.at[t], y1_sem.at[t], side)

    def x2(t):
        arrived(r1x.at[t], x1_sem.at[t])
        at = (t, every, xp, txp)
        dec[at] = (wide(dec, *at) + wide(r1x, t, every, txp)).astype(BF16)
        send(dec.at[t, every, xp, tx], r2x.at[t, 0], x2_sem.at[t], right)
        at = (t, every, xm, txm)
        dec[at] = (wide(dec, *at) + wide(r1x, t, every, txm)).astype(BF16)
        send(dec.at[t, every, xm, tx], r2x.at[t, 1], x2_sem.at[t], left)

    def y2(t):
        arrived(r1y.at[t], y1_sem.at[t])
        o = own(t)
        at = (t, o, every, ty)
        dec[at] = (wide(dec, *at) + wide(r1y, t)).astype(BF16)
        send(dec.at[t, o, xo, typ], r2y.at[t, pl.ds(0, YP)], y2_sem.at[t], right)
        send(dec.at[t, o, xo, tym], r2y.at[t, pl.ds(YP, YT - YP)], y2_sem.at[t], left)

    def x3(t):
        arrived(r2x.at[t], x2_sem.at[t])
        o = 1 - own(t)
        at = (t, o, x, tx)
        dec[at] = (wide(dec, *at) + wide(r2x, t, 0, o) + wide(r2x, t, 1, o)).astype(BF16)
        send(dec.at[at], r3.at[t, tx], r3_sem.at[t], side)

    def y3(t):
        arrived(r2y.at[t], y2_sem.at[t])
        o = own(t)
        at = (t, o, xp, typ)
        dec[at] = (wide(dec, *at) + wide(r2y, t, pl.ds(0, YP))).astype(BF16)
        send(dec.at[t, o, xp, ty], r3.at[t, pl.ds(XT, YT)], r3_sem.at[t], right)
        at = (t, o, xm, tym)
        dec[at] = (wide(dec, *at) + wide(r2y, t, pl.ds(YP, YT - YP))).astype(BF16)
        send(dec.at[t, o, xm, ty], r3.at[t, pl.ds(XT + YT, YT)], r3_sem.at[t], left)

    def z4(t):
        arrived(r3.at[t], r3_sem.at[t])
        o = own(t)
        at = (t, o, x, tx)
        dec[at] = (wide(dec, *at) + wide(r2x, t, 0, o) + wide(r2x, t, 1, o) + wide(r3, t, tx)).astype(BF16)
        at = (t, o, x, ty)
        dec[at] = (wide(dec, *at) + wide(r3, t, ty) + wide(r3, t, pl.ds(XT + YT, YT))).astype(BF16)

        @pl.when(t > 0)
        def _():
            z4_copy(t).start()

        @pl.when(t == 0)
        def _():
            a2a[0] = dec[0, yl, x]

    def z5(t):
        @pl.when(t > 0)
        def _():
            z4_copy(t).wait_recv()

        @pl.when(t == 0)
        def _():
            for load in loads:
                load.wait()

        for k in range(4):
            cols = pl.ds(pl.multiple_of(other(t) * 512 + k * 128, 128), 128)
            average = wide(a2a, t, pl.ds(4 * k, 4)).reshape(64, 128) / F32(8)
            moved = outer_momentum * mom[:, cols] + average
            params = mas[:, cols] - outer_rate * (average + outer_momentum * moved)
            new_momentum[:, cols] = moved
            new_master[:, cols] = params
            ret[t, pl.ds(4 * k, 4)] = params.astype(BF16).reshape(4, 16, 128)

        @pl.when(t > 0)
        def _():
            z5_copy(t).start()

        @pl.when(t == 0)
        def _():
            z5_own().start()

    def ready(t):
        @pl.when(t > 0)
        def _():
            arrived(isl.at[other(t), own(t), x], b_sem.at[t])

        @pl.when(t == 0)
        def _():
            z5_own().wait()

    def gx1(t):
        ready(t)
        spread(isl.at[other(t), own(t), x, tx], gx1_sem.at[t], side)

    def gy1(t):
        at = isl.at[other(t), own(t), x, ty]
        spread(at, gy1_sem.at[t], right)
        spread(at, gy1_sem.at[t], left)

    def gx2(t):
        j = other(t)
        arrived(isl.at[j, 1 - own(t), x, tx], gx1_sem.at[t])
        at = isl.at[j, every, x, tx]
        spread(at, gx2_sem.at[t], right)
        spread(at, gx2_sem.at[t], left)

    def gy2(t):
        j, o = other(t), own(t)
        arrived(isl.at[j, every, x, ty], gy1_sem.at[t])
        spread(isl.at[j, o, xm, typ], gy2_sem.at[t], right)
        spread(isl.at[j, o, xp, tym], gy2_sem.at[t], left)

    def gx3(t):
        j = other(t)
        arrived(isl.at[j, every, pl.ds(0, 2), tx], gx2_sem.at[t])
        spread(isl.at[j, every, xm, txp], gx3_sem, right)
        spread(isl.at[j, every, xp, txm], gx3_sem, left)

    def gy3(t):
        j, o = other(t), own(t)
        arrived(isl.at[j, o, xo, ty], gy2_sem.at[t])
        spread(isl.at[j, o, every, ty], gy3_sem, side)

    barrier = pltpu.get_barrier_semaphore()
    load_e.start()
    load_half(1 - yl, 0).start()
    load_half(yl, UNITS // 2).start()
    friends = [right, left, side] + [partner(jnp.int32(t)) for t in range(1, UNITS)]
    for device in friends:
        pl.semaphore_signal(barrier, inc=1, device_id=device, device_id_type=MESH)
    load_g(1).start()
    load_e.wait()

    def begin(h, _):
        y = h * yl + (1 - h) * (1 - yl)

        @pl.when(h == 0)
        def _():
            load_half(1 - yl, 0).wait()

        @pl.when(h == 1)
        def _():
            load_half(yl, UNITS // 2).wait()

        decode_half(0, y)

        @pl.when(h == 0)
        def _():
            pl.semaphore_wait(barrier, len(friends))
            y1(jnp.int32(0))

        return 0

    lax.fori_loop(0, 2, begin, 0)
    x1(jnp.int32(0))
    for p in range(2, UNITS // 2):
        load_g(p).start()
    for load in loads:
        load.start()

    stages = dict(
        x1=x1, y1=y1, x2=x2, y2=y2, x3=x3, y3=y3, z4=z4, z5=z5, gx1=gx1, gy1=gy1, gx2=gx2, gy2=gy2, gx3=gx3, gy3=gy3
    )

    def step(s, _):
        for name, lag in ORDER:
            if name == "decode":

                @pl.when((lax.rem(s, 2) == 1) & (s < UNITS - 1))
                def _():
                    decode(lax.div(s + 1, 2))

            else:

                @pl.when((s >= lag + (name[1] == "1")) & (s < UNITS + lag))
                def _(lag=lag, stage=stages[name]):
                    stage(s - lag)

        return 0

    lax.fori_loop(0, UNITS + max(lag for _, lag in ORDER), step, 0)

    arrived(isl.at[every, every, xo, tx], gx3_sem)
    arrived(isl.at[every, 0, every, ty], gy3_sem)
    for i, ref in enumerate(
        (dec.at[every, every, every, pl.ds(0, 14)], isl.at[every, every, every, pl.ds(0, 14)], a2a.at[pl.ds(1, 15)], ret.at[pl.ds(1, 15)])
    ):
        remote(ref, ref, i, gx3_sem, right).wait_send()


def order_kernel(layout_far, raw, mas, mom, out, new_master, new_momentum, layout, staged, sems):
    load = pltpu.make_async_copy(layout_far, layout, sems.at[10])
    load.start()
    copies = [pltpu.make_async_copy(mas, new_master, sems.at[8]), pltpu.make_async_copy(mom, new_momentum, sems.at[9])]
    for copy in copies:
        copy.start()
    load.wait()
    for s in range(8):
        l = layout[s]

        def one(j, _, s=s, l=l):
            rows = pl.ds(pl.multiple_of(j * 64, 64), 64)
            for k in range(4):
                staged[s, rows, pl.ds(128 * k, 128)] = raw[j, l // 4, l % 4, pl.ds(4 * k, 4)].reshape(64, 128)
            return 0

        lax.fori_loop(0, UNITS, one, 0)
        copies.append(pltpu.make_async_copy(staged.at[s], out.at[pl.ds(s * 1024, 1024)], sems.at[s]))
        copies[-1].start()
    for copy in copies:
        copy.wait()


def per_device(pseudo_grads, exponents, master, momentum, layout):
    tiles = (TILES, 16, 128)
    vmem = lambda *shape: pltpu.VMEM(shape + (16, 128), BF16)
    dma = lambda *shape: pltpu.SemaphoreType.DMA(shape)
    far = pl.BlockSpec(memory_space=pl.ANY)
    near = pl.BlockSpec(memory_space=pltpu.VMEM)
    results = pl.pallas_call(
        step_kernel,
        out_shape=(
            pltpu.VMEM((UNITS, 2, 4) + tiles, BF16),
            pltpu.VMEM(master.shape, F32),
            pltpu.VMEM(master.shape, F32),
        ),
        in_specs=[far, far, far, far],
        out_specs=(far, near, near),
        scratch_shapes=[
            pltpu.VMEM((UNITS // 2, 8, 128, 512), BF16),
            pltpu.VMEM((4, 8192), jnp.int32),
            vmem(UNITS, 2, 4, TILES),
            vmem(UNITS, 2, XT),
            vmem(UNITS, 4, YT),
            vmem(UNITS, 2, 2, XT),
            vmem(UNITS, YT),
            vmem(UNITS, XT + 2 * YT),
            vmem(UNITS, TILES),
            vmem(UNITS, TILES),
            pltpu.VMEM(master.shape, F32),
            pltpu.VMEM(master.shape, F32),
            dma(UNITS // 2 + 1),
            pltpu.SemaphoreType.DMA,
            dma(2),
            pltpu.SemaphoreType.DMA,
            dma(4),
        ]
        + [dma(UNITS)] * 11
        + [pltpu.SemaphoreType.DMA] * 2,
        compiler_params=pltpu.CompilerParams(
            collective_id=0, has_side_effects=True, vmem_limit_bytes=48 * 2**20
        ),
        name="sum_update_gather",
    )(pseudo_grads.reshape(8, 8, 128, 512), exponents[0].T, master, momentum)

    island, new_master, new_momentum = pl.pallas_call(
        order_kernel,
        out_shape=(
            jax.ShapeDtypeStruct((8192, 512), BF16),
            jax.ShapeDtypeStruct(master.shape, F32),
            jax.ShapeDtypeStruct(master.shape, F32),
        ),
        in_specs=[far, near, near, near],
        out_specs=(far, far, far),
        scratch_shapes=[pltpu.SMEM((8,), jnp.int32), pltpu.VMEM((8, 1024, 512), BF16), dma(11)],
        compiler_params=pltpu.CompilerParams(vmem_limit_bytes=12 * 2**20),
        name="layer_order",
    )(layout, *results)
    return new_master, new_momentum, island


def solution(mesh):
    rows = P(("replica", "fsdp"), None)
    grads = P("replica", None, "fsdp")
    return jax.shard_map(
        per_device,
        mesh=mesh,
        in_specs=(grads, grads, rows, rows, P()),
        out_specs=(rows, rows, P(None, "fsdp")),
        check_vma=False,
    )
```

```python
import jax
import jax.numpy as jnp
from jax import lax
from jax.experimental import pallas as pl
from jax.experimental.pallas import tpu as pltpu
from jax.sharding import PartitionSpec as P

MESH = pl.DeviceIdType.MESH
F32, BF16 = jnp.float32, jnp.bfloat16

outer_rate = 0.7
outer_momentum = 0.9

UNITS = 16
TILES = 16
XT = 9
XP = 5
YT = TILES - XT
YP = 3
YM = XT + YP


ORDER = (
    ("x1", 0), ("y1", 0), ("decode", 0), ("x2", 3), ("y2", 4), ("x3", 6), ("y3", 6), ("z4", 9), ("z5", 12),
    ("gx1", 15), ("gy1", 15), ("gx2", 18), ("gy2", 17), ("gx3", 24), ("gy3", 19),
)


def bit(v, b):
    return lax.rem(lax.div(v, 1 << b), 2)


def flip(a, b):
    return a + b - 2 * a * b


def block_scale(exponents):
    scale = jnp.zeros(exponents.shape, F32)
    for level in range(-6, 2):
        scale = jnp.where(exponents == level, F32(2.0**level), scale)
    return scale


def step_kernel(
    g, exps, master, momentum,
    isl, new_master, new_momentum,
    graw, expt, dec, r1x, r1y, r2x, r2y, r3, a2a, ret, mas, mom,
    go_sem, g_sem, e_sem, m_sem, own_sem, send_sem, x1_sem, y1_sem, x2_sem, y2_sem, r3_sem, a_sem, b_sem,
    gx1_sem, gy1_sem, gx2_sem, gy2_sem, gx3_sem, gy3_sem,
):
    rep, fs = lax.axis_index("replica"), lax.axis_index("fsdp")
    x, yl = lax.rem(rep, 4), lax.div(rep, 4)
    core = lax.rem(fs, 2)
    turn = 2 * core
    xp, xm, xo = lax.rem(x + 1 + turn, 4), lax.rem(x + 3 + turn, 4), lax.rem(x + 2, 4)
    right, left, side = (yl * 4 + xp, fs), (yl * 4 + xm, fs), ((1 - yl) * 4 + x, fs)
    swaps = [(1 - 2 * bit(fs, b)) * (1 << b) for b in range(4)]
    every = slice(None)
    tx, ty = pl.ds(0, XT), pl.ds(XT, YT)
    txp, txm = pl.ds(0, XP), pl.ds(XP, XT - XP)
    typ, tym = pl.ds(XT, YP), pl.ds(YM, YT - YP)

    def other(t):
        return fs + sum(bit(t, b) * swaps[b] for b in range(4))

    def own(t):
        return flip(yl, bit(t, 1))

    def partner(t):
        return (own(t) * 4 + x, other(t))

    def columns(t):
        return pl.ds(pl.multiple_of(other(t) * 512, 512), 512)

    def load_g(p):
        return pltpu.make_async_copy(g.at[:, lax.div(other(2 * p), 2)], graw.at[p], g_sem.at[p])

    def load_half(h, sem):
        at = pl.ds(4 * h, 4)
        return pltpu.make_async_copy(g.at[at, lax.div(fs, 2)], graw.at[0, at], g_sem.at[sem])

    load_e = pltpu.make_async_copy(exps, expt, e_sem)
    barrier = pltpu.get_barrier_semaphore()
    loads = (
        pltpu.make_async_copy(master, mas, m_sem.at[0]),
        pltpu.make_async_copy(momentum, mom, m_sem.at[1]),
    )

    def remote(src, dst, send, recv, device):
        return pltpu.make_async_remote_copy(
            src_ref=src, dst_ref=dst, send_sem=send_sem.at[send], recv_sem=recv, device_id=device, device_id_type=MESH
        )

    def send(src, dst, recv, device):
        remote(src, dst, 0, recv, device).start()

    def spread(ref, recv, device):
        remote(ref, ref, 1, recv, device).start()

    def arrived(ref, recv):
        remote(ref, ref, 0, recv, right).wait_recv()

    def wide(ref, *at):
        return ref[at].astype(F32)

    def z4_copy(t):
        return remote(dec.at[t, own(t), x], a2a.at[t], 2, a_sem.at[t], partner(t))

    def z5_copy(t):
        return remote(ret.at[t], isl.at[fs, yl, x], 3, b_sem.at[t], partner(t))

    def z5_own():
        return pltpu.make_async_copy(ret.at[0], isl.at[fs, yl, x], own_sem)

    lane_block = lax.broadcasted_iota(jnp.int32, (8, 512), 1) // 128
    pick = (lane_block == lax.broadcasted_iota(jnp.int32, (8, 512), 0)).astype(F32)

    def decode_half(p, y):
        base = lax.div(other(2 * p), 2) * 128
        odd = lax.rem(fs, 2)
        for i in range(4):
            rows = pl.ds(pl.multiple_of((4 * y + i) * 1024 + base, 128), 128)
            scale = block_scale(expt[:, rows])
            scale = jnp.concatenate([scale, jnp.zeros((4, 128), F32)], axis=0)
            scales = lax.dot_general(scale, pick, (((0,), (0,)), ((), ())), preferred_element_type=F32).astype(BF16)
            for k in range(4):
                piece = graw[p, 4 * y + i, :, pl.ds(k * 128, 128)] * scales[:, k * 128 : (k + 1) * 128]
                piece = piece.reshape(2, 4, 16, 128)
                for h in range(2):
                    dec[2 * p + flip(odd, h), y, i, pl.ds(4 * k, 4)] = piece[h]

    def decode(p):
        load_g(p).wait()

        def one(y, _):
            decode_half(p, y)
            return 0

        lax.fori_loop(0, 2, one, 0)

    def x1(t):
        send(dec.at[t, every, xo, txp], r1x.at[t, every, txp], x1_sem.at[t], right)
        send(dec.at[t, every, xo, txm], r1x.at[t, every, txm], x1_sem.at[t], left)

    def y1(t):
        send(dec.at[t, 1 - own(t), every, ty], r1y.at[t], y1_sem.at[t], side)

    def x2(t):
        arrived(r1x.at[t], x1_sem.at[t])
        at = (t, every, xp, txp)
        dec[at] = (wide(dec, *at) + wide(r1x, t, every, txp)).astype(BF16)
        send(dec.at[t, every, xp, tx], r2x.at[t, 0], x2_sem.at[t], right)
        at = (t, every, xm, txm)
        dec[at] = (wide(dec, *at) + wide(r1x, t, every, txm)).astype(BF16)
        send(dec.at[t, every, xm, tx], r2x.at[t, 1], x2_sem.at[t], left)

    def y2(t):
        arrived(r1y.at[t], y1_sem.at[t])
        o = own(t)
        at = (t, o, every, ty)
        dec[at] = (wide(dec, *at) + wide(r1y, t)).astype(BF16)
        send(dec.at[t, o, xo, typ], r2y.at[t, pl.ds(0, YP)], y2_sem.at[t], right)
        send(dec.at[t, o, xo, tym], r2y.at[t, pl.ds(YP, YT - YP)], y2_sem.at[t], left)

    def x3(t):
        arrived(r2x.at[t], x2_sem.at[t])
        o = 1 - own(t)
        at = (t, o, x, tx)
        dec[at] = (wide(dec, *at) + wide(r2x, t, 0, o) + wide(r2x, t, 1, o)).astype(BF16)
        send(dec.at[at], r3.at[t, tx], r3_sem.at[t], side)

    def y3(t):
        arrived(r2y.at[t], y2_sem.at[t])
        o = own(t)
        at = (t, o, xp, typ)
        dec[at] = (wide(dec, *at) + wide(r2y, t, pl.ds(0, YP))).astype(BF16)
        send(dec.at[t, o, xp, ty], r3.at[t, pl.ds(XT, YT)], r3_sem.at[t], right)
        at = (t, o, xm, tym)
        dec[at] = (wide(dec, *at) + wide(r2y, t, pl.ds(YP, YT - YP))).astype(BF16)
        send(dec.at[t, o, xm, ty], r3.at[t, pl.ds(XT + YT, YT)], r3_sem.at[t], left)

    def z4(t):
        arrived(r3.at[t], r3_sem.at[t])
        o = own(t)
        at = (t, o, x, tx)
        dec[at] = (wide(dec, *at) + wide(r2x, t, 0, o) + wide(r2x, t, 1, o) + wide(r3, t, tx)).astype(BF16)
        at = (t, o, x, ty)
        dec[at] = (wide(dec, *at) + wide(r3, t, ty) + wide(r3, t, pl.ds(XT + YT, YT))).astype(BF16)

        @pl.when(t > 0)
        def _():
            z4_copy(t).start()

        @pl.when(t == 0)
        def _():
            a2a[0] = dec[0, yl, x]

            @pl.when(core == 1)
            def _():
                pl.semaphore_wait(barrier, 14)
                pl.semaphore_signal(go_sem, inc=1, device_id=(rep, fs - 1), device_id_type=MESH)

            @pl.when(core == 0)
            def _():
                pl.semaphore_wait(go_sem, 1)

    def z5(t):
        @pl.when(t > 0)
        def _():
            z4_copy(t).wait_recv()

        @pl.when(t == 0)
        def _():
            for load in loads:
                load.wait()

        for k in range(4):
            cols = pl.ds(pl.multiple_of(other(t) * 512 + k * 128, 128), 128)
            average = wide(a2a, t, pl.ds(4 * k, 4)).reshape(64, 128) / F32(8)
            moved = outer_momentum * mom[:, cols] + average
            params = mas[:, cols] - outer_rate * (average + outer_momentum * moved)
            new_momentum[:, cols] = moved
            new_master[:, cols] = params
            ret[t, pl.ds(4 * k, 4)] = params.astype(BF16).reshape(4, 16, 128)

        @pl.when(t > 0)
        def _():
            z5_copy(t).start()

        @pl.when(t == 0)
        def _():
            z5_own().start()

    def ready(t):
        @pl.when(t > 0)
        def _():
            arrived(isl.at[other(t), own(t), x], b_sem.at[t])

        @pl.when(t == 0)
        def _():
            z5_own().wait()

    def gx1(t):
        ready(t)
        spread(isl.at[other(t), own(t), x, tx], gx1_sem.at[t], side)

    def gy1(t):
        at = isl.at[other(t), own(t), x, ty]
        spread(at, gy1_sem.at[t], right)
        spread(at, gy1_sem.at[t], left)

    def gx2(t):
        j = other(t)
        arrived(isl.at[j, 1 - own(t), x, tx], gx1_sem.at[t])
        at = isl.at[j, every, x, tx]
        spread(at, gx2_sem.at[t], right)
        spread(at, gx2_sem.at[t], left)

    def gy2(t):
        j, o = other(t), own(t)
        arrived(isl.at[j, every, x, ty], gy1_sem.at[t])
        spread(isl.at[j, o, xm, typ], gy2_sem.at[t], right)
        spread(isl.at[j, o, xp, tym], gy2_sem.at[t], left)

    def gx3(t):
        j = other(t)
        arrived(isl.at[j, every, pl.ds(0, 2), tx], gx2_sem.at[t])
        spread(isl.at[j, every, xm, txp], gx3_sem, right)
        spread(isl.at[j, every, xp, txm], gx3_sem, left)

    def gy3(t):
        j, o = other(t), own(t)
        arrived(isl.at[j, o, xo, ty], gy2_sem.at[t])
        spread(isl.at[j, o, every, ty], gy3_sem, side)

    load_e.start()
    load_half(1 - yl, 0).start()
    load_half(yl, UNITS // 2).start()
    for where, _ in (right, left, side):
        pl.semaphore_signal(barrier, inc=1, device_id=(where, fs - core), device_id_type=MESH)
    for t in range(2, UNITS, 2):
        where, there = partner(jnp.int32(t))
        pl.semaphore_signal(barrier, inc=1, device_id=(where, there - core + 1), device_id_type=MESH)

    @pl.when(core == 1)
    def _():
        pl.semaphore_signal(barrier, inc=1, device_id=(rep, fs - 1), device_id_type=MESH)

    load_g(1).start()
    load_e.wait()

    def begin(h, _):
        y = h * yl + (1 - h) * (1 - yl)

        @pl.when(h == 0)
        def _():
            load_half(1 - yl, 0).wait()

        @pl.when(h == 1)
        def _():
            load_half(yl, UNITS // 2).wait()

        decode_half(0, y)

        @pl.when(h == 0)
        def _():
            @pl.when(core == 0)
            def _():
                pl.semaphore_wait(barrier, 7)
                pl.semaphore_signal(go_sem, inc=1, device_id=(rep, fs + 1), device_id_type=MESH)

            @pl.when(core == 1)
            def _():
                pl.semaphore_wait(go_sem, 1)

            y1(jnp.int32(0))

        return 0

    lax.fori_loop(0, 2, begin, 0)
    x1(jnp.int32(0))
    for p in range(2, UNITS // 2):
        load_g(p).start()
    for load in loads:
        load.start()

    stages = dict(
        x1=x1, y1=y1, x2=x2, y2=y2, x3=x3, y3=y3, z4=z4, z5=z5, gx1=gx1, gy1=gy1, gx2=gx2, gy2=gy2, gx3=gx3, gy3=gy3
    )

    def step(s, _):
        for name, lag in ORDER:
            if name == "decode":

                @pl.when((lax.rem(s, 2) == 1) & (s < UNITS - 1))
                def _():
                    decode(lax.div(s + 1, 2))

            else:

                @pl.when((s >= lag + (name[1] == "1")) & (s < UNITS + lag))
                def _(lag=lag, stage=stages[name]):
                    stage(s - lag)

        return 0

    lax.fori_loop(0, UNITS + max(lag for _, lag in ORDER), step, 0)

    arrived(isl.at[every, every, xo, tx], gx3_sem)
    arrived(isl.at[every, 0, every, ty], gy3_sem)
    for i, ref in enumerate(
        (dec.at[every, every, every, pl.ds(0, 14)], isl.at[every, every, every, pl.ds(0, 14)], a2a.at[pl.ds(1, 15)], ret.at[pl.ds(1, 15)])
    ):
        remote(ref, ref, i, gx3_sem, right).wait_send()


def order_kernel(layout_far, raw, mas, mom, out, new_master, new_momentum, layout, staged, sems):
    load = pltpu.make_async_copy(layout_far, layout, sems.at[10])
    load.start()
    copies = [pltpu.make_async_copy(mas, new_master, sems.at[8]), pltpu.make_async_copy(mom, new_momentum, sems.at[9])]
    for copy in copies:
        copy.start()
    load.wait()
    for s in range(8):
        l = layout[s]

        def one(j, _, s=s, l=l):
            rows = pl.ds(pl.multiple_of(j * 64, 64), 64)
            for k in range(4):
                staged[s, rows, pl.ds(128 * k, 128)] = raw[j, l // 4, l % 4, pl.ds(4 * k, 4)].reshape(64, 128)
            return 0

        lax.fori_loop(0, UNITS, one, 0)
        copies.append(pltpu.make_async_copy(staged.at[s], out.at[pl.ds(s * 1024, 1024)], sems.at[s]))
        copies[-1].start()
    for copy in copies:
        copy.wait()


def per_device(pseudo_grads, exponents, master, momentum, layout):
    tiles = (TILES, 16, 128)
    vmem = lambda *shape: pltpu.VMEM(shape + (16, 128), BF16)
    dma = lambda *shape: pltpu.SemaphoreType.DMA(shape)
    far = pl.BlockSpec(memory_space=pl.ANY)
    near = pl.BlockSpec(memory_space=pltpu.VMEM)
    results = pl.pallas_call(
        step_kernel,
        out_shape=(
            pltpu.VMEM((UNITS, 2, 4) + tiles, BF16),
            pltpu.VMEM(master.shape, F32),
            pltpu.VMEM(master.shape, F32),
        ),
        in_specs=[far, far, far, far],
        out_specs=(far, near, near),
        scratch_shapes=[
            pltpu.VMEM((UNITS // 2, 8, 128, 512), BF16),
            pltpu.VMEM((4, 8192), jnp.int32),
            vmem(UNITS, 2, 4, TILES),
            vmem(UNITS, 2, XT),
            vmem(UNITS, 4, YT),
            vmem(UNITS, 2, 2, XT),
            vmem(UNITS, YT),
            vmem(UNITS, XT + 2 * YT),
            vmem(UNITS, TILES),
            vmem(UNITS, TILES),
            pltpu.VMEM(master.shape, F32),
            pltpu.VMEM(master.shape, F32),
            pltpu.SemaphoreType.REGULAR,
            dma(UNITS // 2 + 1),
            pltpu.SemaphoreType.DMA,
            dma(2),
            pltpu.SemaphoreType.DMA,
            dma(4),
        ]
        + [dma(UNITS)] * 11
        + [pltpu.SemaphoreType.DMA] * 2,
        compiler_params=pltpu.CompilerParams(
            collective_id=0, has_side_effects=True, vmem_limit_bytes=48 * 2**20
        ),
        name="sum_update_gather",
    )(pseudo_grads.reshape(8, 8, 128, 512), exponents[0].T, master, momentum)

    island, new_master, new_momentum = pl.pallas_call(
        order_kernel,
        out_shape=(
            jax.ShapeDtypeStruct((8192, 512), BF16),
            jax.ShapeDtypeStruct(master.shape, F32),
            jax.ShapeDtypeStruct(master.shape, F32),
        ),
        in_specs=[far, near, near, near],
        out_specs=(far, far, far),
        scratch_shapes=[pltpu.SMEM((8,), jnp.int32), pltpu.VMEM((8, 1024, 512), BF16), dma(11)],
        compiler_params=pltpu.CompilerParams(vmem_limit_bytes=12 * 2**20),
        name="layer_order",
    )(layout, *results)
    return new_master, new_momentum, island


def solution(mesh):
    rows = P(("replica", "fsdp"), None)
    grads = P("replica", None, "fsdp")
    return jax.shard_map(
        per_device,
        mesh=mesh,
        in_specs=(grads, grads, rows, rows, P()),
        out_specs=(rows, rows, P(None, "fsdp")),
        check_vma=False,
    )
```

```python
import jax
import jax.numpy as jnp
from jax import lax
from jax.experimental import pallas as pl
from jax.experimental.pallas import tpu as pltpu
from jax.sharding import PartitionSpec as P

MESH = pl.DeviceIdType.MESH
F32, BF16 = jnp.float32, jnp.bfloat16

outer_rate = 0.7
outer_momentum = 0.9

UNITS = 16
TILES = 16
XT = 9
XP = 5
YT = TILES - XT
YP = 3
YM = XT + YP
WINDOW = 8


ORDER = (
    ("x1", 0), ("y1", 0), ("decode", 0), ("x2", 3), ("y2", 4), ("x3", 6), ("y3", 6), ("z4", 9), ("z5", 12),
    ("gx1", 15), ("gy1", 15), ("gx2", 18), ("gy2", 17), ("gx3", 24), ("gy3", 19),
)


def bit(v, b):
    return lax.rem(lax.div(v, 1 << b), 2)


def flip(a, b):
    return a + b - 2 * a * b


def block_scale(exponents):
    scale = jnp.zeros(exponents.shape, F32)
    for level in range(-6, 2):
        scale = jnp.where(exponents == level, F32(2.0**level), scale)
    return scale


def step_kernel(
    g, exps, master, momentum,
    isl, new_master, new_momentum,
    graw, expt, dec, r1x, r1y, r2x, r2y, r3, a2a, ret, mas, mom,
    go_sem, g_sem, e_sem, m_sem, own_sem, send_sem, x1_sem, y1_sem, x2_sem, y2_sem, r3_sem, a_sem, b_sem,
    gx1_sem, gy1_sem, gx2_sem, gy2_sem, gx3_sem, gy3_sem,
):
    rep, fs = lax.axis_index("replica"), lax.axis_index("fsdp")
    x, yl = lax.rem(rep, 4), lax.div(rep, 4)
    core = lax.rem(fs, 2)
    turn = 2 * core
    xp, xm, xo = lax.rem(x + 1 + turn, 4), lax.rem(x + 3 + turn, 4), lax.rem(x + 2, 4)
    right, left, side = (yl * 4 + xp, fs), (yl * 4 + xm, fs), ((1 - yl) * 4 + x, fs)
    swaps = [(1 - 2 * bit(fs, b)) * (1 << b) for b in range(4)]
    every = slice(None)
    tx, ty = pl.ds(0, XT), pl.ds(XT, YT)
    txp, txm = pl.ds(0, XP), pl.ds(XP, XT - XP)
    typ, tym = pl.ds(XT, YP), pl.ds(YM, YT - YP)

    def other(t):
        return fs + sum(bit(t, b) * swaps[b] for b in range(4))

    def own(t):
        return flip(yl, bit(t, 1))

    def partner(t):
        return (own(t) * 4 + x, other(t))

    def columns(t):
        return pl.ds(pl.multiple_of(other(t) * 512, 512), 512)

    def load_g(p):
        return pltpu.make_async_copy(g.at[:, lax.div(other(2 * p), 2)], graw.at[p], g_sem.at[p])

    def load_half(h, sem):
        at = pl.ds(4 * h, 4)
        return pltpu.make_async_copy(g.at[at, lax.div(fs, 2)], graw.at[0, at], g_sem.at[sem])

    load_e = pltpu.make_async_copy(exps, expt, e_sem)
    barrier = pltpu.get_barrier_semaphore()
    loads = (
        pltpu.make_async_copy(master, mas, m_sem.at[0]),
        pltpu.make_async_copy(momentum, mom, m_sem.at[1]),
    )

    def remote(src, dst, send, recv, device):
        return pltpu.make_async_remote_copy(
            src_ref=src, dst_ref=dst, send_sem=send_sem.at[send], recv_sem=recv, device_id=device, device_id_type=MESH
        )

    def send(src, dst, recv, device):
        remote(src, dst, 0, recv, device).start()

    def spread(ref, recv, device):
        remote(ref, ref, 1, recv, device).start()

    def arrived(ref, recv):
        remote(ref, ref, 0, recv, right).wait_recv()

    def wide(ref, *at):
        return ref[at].astype(F32)

    def z4_copy(t):
        return remote(dec.at[t, own(t), x], a2a.at[t], 2, a_sem.at[t], partner(t))

    def z5_copy(t):
        return remote(ret.at[t], isl.at[fs, yl, x], 3, b_sem.at[t], partner(t))

    def z5_own():
        return pltpu.make_async_copy(ret.at[0], isl.at[fs, yl, x], own_sem)

    lane_block = lax.broadcasted_iota(jnp.int32, (8, 512), 1) // 128
    pick = (lane_block == lax.broadcasted_iota(jnp.int32, (8, 512), 0)).astype(F32)

    def decode_half(p, y):
        base = lax.div(other(2 * p), 2) * 128
        odd = lax.rem(fs, 2)
        for i in range(4):
            rows = pl.ds(pl.multiple_of((4 * y + i) * 1024 + base, 128), 128)
            scale = block_scale(expt[:, rows])
            scale = jnp.concatenate([scale, jnp.zeros((4, 128), F32)], axis=0)
            scales = lax.dot_general(scale, pick, (((0,), (0,)), ((), ())), preferred_element_type=F32).astype(BF16)
            for k in range(4):
                piece = graw[p, 4 * y + i, :, pl.ds(k * 128, 128)] * scales[:, k * 128 : (k + 1) * 128]
                piece = piece.reshape(2, 4, 16, 128)
                for h in range(2):
                    dec[2 * p + flip(odd, h), y, i, pl.ds(4 * k, 4)] = piece[h]

    def decode(p):
        load_g(p).wait()

        def one(y, _):
            decode_half(p, y)
            return 0

        lax.fori_loop(0, 2, one, 0)

    def x1(t):
        send(dec.at[t, every, xo, txp], r1x.at[t, every, txp], x1_sem.at[lax.rem(t, WINDOW)], right)
        send(dec.at[t, every, xo, txm], r1x.at[t, every, txm], x1_sem.at[lax.rem(t, WINDOW)], left)

    def y1(t):
        send(dec.at[t, 1 - own(t), every, ty], r1y.at[t], y1_sem.at[t], side)

    def x2(t):
        arrived(r1x.at[t], x1_sem.at[lax.rem(t, WINDOW)])
        at = (t, every, xp, txp)
        dec[at] = (wide(dec, *at) + wide(r1x, t, every, txp)).astype(BF16)
        send(dec.at[t, every, xp, tx], r2x.at[t, 0], x2_sem.at[lax.rem(t, WINDOW)], right)
        at = (t, every, xm, txm)
        dec[at] = (wide(dec, *at) + wide(r1x, t, every, txm)).astype(BF16)
        send(dec.at[t, every, xm, tx], r2x.at[t, 1], x2_sem.at[lax.rem(t, WINDOW)], left)

    def y2(t):
        arrived(r1y.at[t], y1_sem.at[t])
        o = own(t)
        at = (t, o, every, ty)
        dec[at] = (wide(dec, *at) + wide(r1y, t)).astype(BF16)
        send(dec.at[t, o, xo, typ], r2y.at[t, pl.ds(0, YP)], y2_sem.at[lax.rem(t, WINDOW)], right)
        send(dec.at[t, o, xo, tym], r2y.at[t, pl.ds(YP, YT - YP)], y2_sem.at[lax.rem(t, WINDOW)], left)

    def x3(t):
        arrived(r2x.at[t], x2_sem.at[lax.rem(t, WINDOW)])
        o = 1 - own(t)
        at = (t, o, x, tx)
        dec[at] = (wide(dec, *at) + wide(r2x, t, 0, o) + wide(r2x, t, 1, o)).astype(BF16)
        send(dec.at[at], r3.at[t, tx], r3_sem.at[lax.rem(t, WINDOW)], side)

    def y3(t):
        arrived(r2y.at[t], y2_sem.at[lax.rem(t, WINDOW)])
        o = own(t)
        at = (t, o, xp, typ)
        dec[at] = (wide(dec, *at) + wide(r2y, t, pl.ds(0, YP))).astype(BF16)
        send(dec.at[t, o, xp, ty], r3.at[t, pl.ds(XT, YT)], r3_sem.at[lax.rem(t, WINDOW)], right)
        at = (t, o, xm, tym)
        dec[at] = (wide(dec, *at) + wide(r2y, t, pl.ds(YP, YT - YP))).astype(BF16)
        send(dec.at[t, o, xm, ty], r3.at[t, pl.ds(XT + YT, YT)], r3_sem.at[lax.rem(t, WINDOW)], left)

    def z4(t):
        arrived(r3.at[t], r3_sem.at[lax.rem(t, WINDOW)])
        o = own(t)
        at = (t, o, x, tx)
        dec[at] = (wide(dec, *at) + wide(r2x, t, 0, o) + wide(r2x, t, 1, o) + wide(r3, t, tx)).astype(BF16)
        at = (t, o, x, ty)
        dec[at] = (wide(dec, *at) + wide(r3, t, ty) + wide(r3, t, pl.ds(XT + YT, YT))).astype(BF16)

        @pl.when(t > 0)
        def _():
            z4_copy(t).start()

        @pl.when(t == 0)
        def _():
            a2a[0] = dec[0, yl, x]

            @pl.when(core == 1)
            def _():
                pl.semaphore_wait(barrier, 14)
                pl.semaphore_signal(go_sem, inc=1, device_id=(rep, fs - 1), device_id_type=MESH)

            @pl.when(core == 0)
            def _():
                pl.semaphore_wait(go_sem, 1)

    def z5(t):
        @pl.when(t > 0)
        def _():
            z4_copy(t).wait_recv()

        @pl.when(t == 0)
        def _():
            for load in loads:
                load.wait()

        for k in range(4):
            cols = pl.ds(pl.multiple_of(other(t) * 512 + k * 128, 128), 128)
            average = wide(a2a, t, pl.ds(4 * k, 4)).reshape(64, 128) / F32(8)
            moved = outer_momentum * mom[:, cols] + average
            params = mas[:, cols] - outer_rate * (average + outer_momentum * moved)
            new_momentum[:, cols] = moved
            new_master[:, cols] = params
            ret[t, pl.ds(4 * k, 4)] = params.astype(BF16).reshape(4, 16, 128)

        @pl.when(t > 0)
        def _():
            z5_copy(t).start()

        @pl.when(t == 0)
        def _():
            z5_own().start()

    def ready(t):
        @pl.when(t > 0)
        def _():
            arrived(isl.at[other(t), own(t), x], b_sem.at[t])

        @pl.when(t == 0)
        def _():
            z5_own().wait()

    def gx1(t):
        ready(t)
        spread(isl.at[other(t), own(t), x, tx], gx1_sem.at[lax.rem(t, WINDOW)], side)

    def gy1(t):
        at = isl.at[other(t), own(t), x, ty]
        spread(at, gy1_sem.at[lax.rem(t, WINDOW)], right)
        spread(at, gy1_sem.at[lax.rem(t, WINDOW)], left)

    def gx2(t):
        j = other(t)
        arrived(isl.at[j, 1 - own(t), x, tx], gx1_sem.at[lax.rem(t, WINDOW)])
        at = isl.at[j, every, x, tx]
        spread(at, gx2_sem.at[t], right)
        spread(at, gx2_sem.at[t], left)

    def gy2(t):
        j, o = other(t), own(t)
        arrived(isl.at[j, every, x, ty], gy1_sem.at[lax.rem(t, WINDOW)])
        spread(isl.at[j, o, xm, typ], gy2_sem.at[lax.rem(t, WINDOW)], right)
        spread(isl.at[j, o, xp, tym], gy2_sem.at[lax.rem(t, WINDOW)], left)

    def gx3(t):
        j = other(t)
        arrived(isl.at[j, every, pl.ds(0, 2), tx], gx2_sem.at[t])
        spread(isl.at[j, every, xm, txp], gx3_sem, right)
        spread(isl.at[j, every, xp, txm], gx3_sem, left)

    def gy3(t):
        j, o = other(t), own(t)
        arrived(isl.at[j, o, xo, ty], gy2_sem.at[lax.rem(t, WINDOW)])
        spread(isl.at[j, o, every, ty], gy3_sem, side)

    load_e.start()
    load_half(1 - yl, 0).start()
    load_half(yl, UNITS // 2).start()
    for where, _ in (right, left, side):
        pl.semaphore_signal(barrier, inc=1, device_id=(where, fs - core), device_id_type=MESH)
    for t in range(2, UNITS, 2):
        where, there = partner(jnp.int32(t))
        pl.semaphore_signal(barrier, inc=1, device_id=(where, there - core + 1), device_id_type=MESH)

    @pl.when(core == 1)
    def _():
        pl.semaphore_signal(barrier, inc=1, device_id=(rep, fs - 1), device_id_type=MESH)

    load_g(1).start()
    load_e.wait()

    def begin(h, _):
        y = h * yl + (1 - h) * (1 - yl)

        @pl.when(h == 0)
        def _():
            load_half(1 - yl, 0).wait()

        @pl.when(h == 1)
        def _():
            load_half(yl, UNITS // 2).wait()

        decode_half(0, y)

        @pl.when(h == 0)
        def _():
            @pl.when(core == 0)
            def _():
                pl.semaphore_wait(barrier, 7)
                pl.semaphore_signal(go_sem, inc=1, device_id=(rep, fs + 1), device_id_type=MESH)

            @pl.when(core == 1)
            def _():
                pl.semaphore_wait(go_sem, 1)

            y1(jnp.int32(0))
            y1(jnp.int32(1))

        return 0

    lax.fori_loop(0, 2, begin, 0)
    x1(jnp.int32(0))
    for p in range(2, UNITS // 2):
        load_g(p).start()
    for load in loads:
        load.start()

    stages = dict(
        x1=x1, y1=y1, x2=x2, y2=y2, x3=x3, y3=y3, z4=z4, z5=z5, gx1=gx1, gy1=gy1, gx2=gx2, gy2=gy2, gx3=gx3, gy3=gy3
    )

    def step(s, _):
        for name, lag in ORDER:
            if name == "decode":

                @pl.when((lax.rem(s, 2) == 1) & (s < UNITS - 1))
                def _():
                    decode(lax.div(s + 1, 2))

            else:

                @pl.when((s >= lag + {"x1": 1, "y1": 2}.get(name, 0)) & (s < UNITS + lag))
                def _(lag=lag, stage=stages[name]):
                    stage(s - lag)

        return 0

    lax.fori_loop(0, UNITS + max(lag for _, lag in ORDER), step, 0)

    arrived(isl.at[every, every, xo, tx], gx3_sem)
    arrived(isl.at[every, 0, every, ty], gy3_sem)
    for i, ref in enumerate(
        (dec.at[every, every, every, pl.ds(0, 14)], isl.at[every, every, every, pl.ds(0, 14)], a2a.at[pl.ds(1, 15)], ret.at[pl.ds(1, 15)])
    ):
        remote(ref, ref, i, gx3_sem, right).wait_send()


def order_kernel(layout_far, raw, mas, mom, out, new_master, new_momentum, layout, staged, sems):
    load = pltpu.make_async_copy(layout_far, layout, sems.at[10])
    load.start()
    copies = [pltpu.make_async_copy(mas, new_master, sems.at[8]), pltpu.make_async_copy(mom, new_momentum, sems.at[9])]
    for copy in copies:
        copy.start()
    load.wait()
    for s in range(8):
        l = layout[s]

        def one(j, _, s=s, l=l):
            rows = pl.ds(pl.multiple_of(j * 64, 64), 64)
            for k in range(4):
                staged[s, rows, pl.ds(128 * k, 128)] = raw[j, l // 4, l % 4, pl.ds(4 * k, 4)].reshape(64, 128)
            return 0

        lax.fori_loop(0, UNITS, one, 0)
        copies.append(pltpu.make_async_copy(staged.at[s], out.at[pl.ds(s * 1024, 1024)], sems.at[s]))
        copies[-1].start()
    for copy in copies:
        copy.wait()


def per_device(pseudo_grads, exponents, master, momentum, layout):
    tiles = (TILES, 16, 128)
    vmem = lambda *shape: pltpu.VMEM(shape + (16, 128), BF16)
    dma = lambda *shape: pltpu.SemaphoreType.DMA(shape)
    far = pl.BlockSpec(memory_space=pl.ANY)
    near = pl.BlockSpec(memory_space=pltpu.VMEM)
    results = pl.pallas_call(
        step_kernel,
        out_shape=(
            pltpu.VMEM((UNITS, 2, 4) + tiles, BF16),
            pltpu.VMEM(master.shape, F32),
            pltpu.VMEM(master.shape, F32),
        ),
        in_specs=[far, far, far, far],
        out_specs=(far, near, near),
        scratch_shapes=[
            pltpu.VMEM((UNITS // 2, 8, 128, 512), BF16),
            pltpu.VMEM((4, 8192), jnp.int32),
            vmem(UNITS, 2, 4, TILES),
            vmem(UNITS, 2, XT),
            vmem(UNITS, 4, YT),
            vmem(UNITS, 2, 2, XT),
            vmem(UNITS, YT),
            vmem(UNITS, XT + 2 * YT),
            vmem(UNITS, TILES),
            vmem(UNITS, TILES),
            pltpu.VMEM(master.shape, F32),
            pltpu.VMEM(master.shape, F32),
            pltpu.SemaphoreType.REGULAR,
            dma(UNITS // 2 + 1),
            pltpu.SemaphoreType.DMA,
            dma(2),
            pltpu.SemaphoreType.DMA,
            dma(4),
        ]
        + [dma(WINDOW), dma(UNITS)]
        + [dma(WINDOW)] * 3
        + [dma(UNITS)] * 2
        + [dma(WINDOW)] * 2
        + [dma(UNITS)]
        + [dma(WINDOW)]
        + [pltpu.SemaphoreType.DMA] * 2,
        compiler_params=pltpu.CompilerParams(
            collective_id=0, has_side_effects=True, vmem_limit_bytes=48 * 2**20
        ),
        name="sum_update_gather",
    )(pseudo_grads.reshape(8, 8, 128, 512), exponents[0].T, master, momentum)

    island, new_master, new_momentum = pl.pallas_call(
        order_kernel,
        out_shape=(
            jax.ShapeDtypeStruct((8192, 512), BF16),
            jax.ShapeDtypeStruct(master.shape, F32),
            jax.ShapeDtypeStruct(master.shape, F32),
        ),
        in_specs=[far, near, near, near],
        out_specs=(far, far, far),
        scratch_shapes=[pltpu.SMEM((8,), jnp.int32), pltpu.VMEM((8, 1024, 512), BF16), dma(11)],
        compiler_params=pltpu.CompilerParams(vmem_limit_bytes=12 * 2**20),
        name="layer_order",
    )(layout, *results)
    return new_master, new_momentum, island


def solution(mesh):
    rows = P(("replica", "fsdp"), None)
    grads = P("replica", None, "fsdp")
    return jax.shard_map(
        per_device,
        mesh=mesh,
        in_specs=(grads, grads, rows, rows, P()),
        out_specs=(rows, rows, P(None, "fsdp")),
        check_vma=False,
    )
```
